256 devices in a mesh: hist: 16 (over y, z_hi, core), mp: 16 (over x, z_lo).
Axes of the slice: x: 4, y: 4, z: 8 (z_hi: 2, z_lo: 4; z = z_hi * 4 + z_lo), core: 2. Of those that a mesh axis runs over, the one named last changes fastest.
Arguments:
- history_ids: int32 [8192], P('hist'), may hold values from 0 to 255
- latent_offsets: int32 [1024], P('hist'), may hold values from 0 to 8191, as said below
- byte_table: bfloat16 [256, 4096], replicated, may hold values from -6 to 6
- w_query: bfloat16 [4096, 4096], P(None, 'mp')
- w_key: bfloat16 [4096, 4096], P(None, 'mp')
- w_value: bfloat16 [4096, 4096], P(None, 'mp'), may hold values from -0.09375 to 0.09375
- w_out: bfloat16 [4096, 4096], P('mp'), may hold values from -0.125 to 0.125
- norm_gain: bfloat16 [4096], replicated, may hold values from 0.099609375 to 1.8984375
- w_self_query: bfloat16 [4096, 4096], P('hist', 'mp')
- w_self_key: bfloat16 [4096, 4096], P('hist', 'mp')
- w_self_value: bfloat16 [4096, 4096], P('hist', 'mp'), may hold values from -0.09375 to 0.09375
- w_self_out: bfloat16 [4096, 4096], P('mp', 'hist'), may hold values from -0.125 to 0.125
Outputs:
- latent_out: bfloat16 [1024, 4096], P('hist', 'mp')
The draws below stay inside these ranges and needn't reach their ends.
Inputs may be any that keep to these rules, and one draw needn't show every extreme that they name: `latent_offsets`: strictly rising; latent i lies at or after position i * 8 and before (i + 1) * 8; the first is 0 and the last 8191.
All inputs are finite; a program needn't handle non-finite values.
Results may differ from the reference program's by a relative error of at most 0.035.
Values may be sent and summed in bfloat16 or wider, within the bound.
A program may use at most 64 MiB of HBM per device.

```python
import math
import jax
import jax.numpy as jnp
from jax import lax

D = 4096
HEADS = 32
VOCAB = 256
STRIDE = 8
HEAD_DIM = 128
H = 8192
Q = 1024
N_MP = 16


def shared_draw(key, salt):
    return jax.random.normal(jax.random.fold_in(key, salt), (D, D), jnp.float32)


def draw_latent_offsets(key, part):
    key = jax.random.fold_in(key, 7)
    latent_index = jnp.arange(Q, dtype=jnp.int32)
    jitter = jax.random.randint(key, (Q,), 0, STRIDE, dtype=jnp.int32)
    offsets_drawn = latent_index * STRIDE + jitter
    offsets_drawn = jnp.where(latent_index == 0, 0, offsets_drawn)
    offsets_drawn = jnp.where(latent_index == Q - 1, H - 1, offsets_drawn)
    return offsets_drawn.astype(jnp.int32)


def draw_w_key(key, part):
    common = shared_draw(key, 101)
    return (common / math.sqrt(D)).astype(jnp.bfloat16)


def draw_w_query(key, part):
    key = jax.random.fold_in(key, 13)
    private = jax.random.normal(key, (D, D), jnp.float32)
    return (private / math.sqrt(D)).astype(jnp.bfloat16)


def draw_w_self_key(key, part):
    common = shared_draw(key, 202)
    return (common / math.sqrt(D)).astype(jnp.bfloat16)


def draw_w_self_query(key, part):
    key = jax.random.fold_in(key, 15)
    private = jax.random.normal(key, (D, D), jnp.float32)
    return (private / math.sqrt(D)).astype(jnp.bfloat16)


def set_ends(drawn, key, least, largest):
    index_at = [jax.random.randint(jax.random.fold_in(key, axis), (), 0, length) for axis, length in enumerate(drawn.shape)]
    main_axis = drawn.shape.index(max(drawn.shape))
    beside = index_at[:main_axis] + [(index_at[main_axis] + 1) % drawn.shape[main_axis]] + index_at[main_axis + 1:]
    return drawn.at[tuple(index_at)].set(least).at[tuple(beside)].set(largest)


def spiked(array, rng, source, target, blocks, factor):
    def block_of(position):
        return (jnp.arange(array.shape[position]) // (array.shape[position] // blocks)).reshape((-1,) + (1,) * (array.ndim - 1 - position))

    near = jax.random.permutation(rng, blocks)[block_of(target)]
    second = (block_of(target) + blocks // 2) % blocks
    return jnp.where((block_of(source) == near) | (block_of(source) == second), factor * array, array)


def levels(rng, extent, cuts, least, high):
    def one(axis_at, shards_of):
        steps = jax.random.uniform(jax.random.fold_in(jax.random.fold_in(rng, 6), axis_at), (shards_of,), jnp.float32, least / len(cuts), high / len(cuts))
        return jnp.repeat(jnp.exp(steps), extent[axis_at] // shards_of).reshape((-1,) + (1,) * (len(extent) - axis_at - 1))

    loudness = one(*cuts[0])
    for cut in cuts[1:]:
        loudness = loudness * one(*cut)
    return loudness


def gaussian(key, extent, spread, reach, pieces=(), held_as=jnp.bfloat16):
    gain = levels(key, extent, pieces, -0.22, 0.18) if pieces else 1.0
    array = jax.random.normal(key, extent, jnp.float32) * spread * gain
    return jnp.minimum(jnp.maximum(array, -reach), reach).astype(held_as)


def bell_draw_with(rng, extent, width, most, shards, heavy, kind=jnp.bfloat16):
    array = width * jax.random.normal(rng, extent, jnp.float32)
    if shards:
        array = array * levels(rng, extent, shards, -0.22, 0.18)
    return jnp.clip(spiked(array, jax.random.fold_in(rng, 3), *heavy), -most, most).astype(kind)


def setup_inputs(seed: int = 0) -> dict:
    streams_of = jax.random.split(jax.random.key(seed), 13)
    history_ids = set_ends(jax.random.randint(streams_of[0], (H,), 0, VOCAB), jax.random.fold_in(streams_of[0], 1), 0, VOCAB - 1).astype(jnp.int32)
    latent_offsets = draw_latent_offsets(jax.random.fold_in(streams_of[12], 71), 0)
    byte_table = gaussian(streams_of[2], (VOCAB, D), 1.0, 6.0)
    w_query = draw_w_query(jax.random.fold_in(streams_of[12], 71), 0)
    w_key = draw_w_key(jax.random.fold_in(streams_of[12], 71), 0)
    w_value = gaussian(streams_of[5], (D, D), D ** -0.5, 0.09375, ((1, 16),))
    w_out = bell_draw_with(streams_of[6], (D, D), D ** -0.5, 0.125, ((0, 16),), (0, 1, 16, 2.0))
    norm_gain = jnp.clip(1.0 + 0.18 * jax.random.normal(streams_of[7], (D,), jnp.float32), 0.099609375, 1.8984375).astype(jnp.bfloat16)
    w_self_query = draw_w_self_query(jax.random.fold_in(streams_of[12], 71), 0)
    w_self_key = draw_w_self_key(jax.random.fold_in(streams_of[12], 71), 0)
    w_self_value = gaussian(streams_of[10], (D, D), D ** -0.5, 0.09375, ((0, 16), (1, 16)))
    w_self_out = bell_draw_with(streams_of[11], (D, D), D ** -0.5, 0.125, ((0, 16), (1, 16)), (0, 1, 16, 2.0))
    return {"history_ids": history_ids, "latent_offsets": latent_offsets, "byte_table": byte_table, "w_query": w_query, "w_key": w_key, "w_value": w_value, "w_out": w_out, "norm_gain": norm_gain, "w_self_query": w_self_query, "w_self_key": w_self_key, "w_self_value": w_self_value, "w_self_out": w_self_out}


def attention(queries, key_block, value_block, allowed):
    row_count = queries.shape[0]
    key_count = key_block.shape[0]
    query_heads = queries.reshape(row_count, HEADS, HEAD_DIM).transpose(1, 0, 2)
    key_heads = key_block.reshape(key_count, HEADS, HEAD_DIM).transpose(1, 0, 2)
    value_heads = value_block.reshape(key_count, HEADS, HEAD_DIM).transpose(1, 0, 2)

    def single_head(operands):
        query_one, key_one, value_one = operands
        scores = jnp.dot(query_one, key_one.T, preferred_element_type=jnp.float32) * (1.0 / math.sqrt(HEAD_DIM))
        scores = jnp.where(allowed, scores, -1e+30)
        row_top = lax.optimization_barrier(jnp.max(scores, axis=1, keepdims=True))
        weights = jnp.where(allowed, jnp.exp(scores - row_top), 0.0)
        totals = lax.optimization_barrier(jnp.sum(weights, axis=1, keepdims=True))
        return jnp.dot(weights.astype(jnp.bfloat16), value_one, preferred_element_type=jnp.float32) / totals
    outputs = lax.map(single_head, (query_heads, key_heads, value_heads))
    return outputs.transpose(1, 0, 2).reshape(row_count, HEADS * HEAD_DIM).astype(jnp.bfloat16)

def grouped_product(left, weight):
    row_count = left.shape[0]
    group_width = D // N_MP
    accumulated = jnp.zeros((row_count, D), jnp.float32)
    for group in range(N_MP):
        piece = jnp.dot(left[:, group * group_width:(group + 1) * group_width], weight[group * group_width:(group + 1) * group_width], preferred_element_type=jnp.float32)
        accumulated = accumulated + lax.optimization_barrier(piece.astype(jnp.bfloat16)).astype(jnp.float32)
    return accumulated

def reference(history_ids, latent_offsets, byte_table, w_query, w_key, w_value, w_out, norm_gain, w_self_query, w_self_key, w_self_value, w_self_out):
    embedded = jnp.take(byte_table, history_ids, axis=0)
    hist_keys = jnp.dot(embedded, w_key, preferred_element_type=jnp.float32).astype(jnp.bfloat16)
    hist_values = jnp.dot(embedded, w_value, preferred_element_type=jnp.float32).astype(jnp.bfloat16)
    latent_embed = jnp.take(embedded, latent_offsets, axis=0)
    latent_queries = jnp.dot(latent_embed, w_query, preferred_element_type=jnp.float32).astype(jnp.bfloat16)
    positions = jnp.arange(H, dtype=jnp.int32)
    allowed = positions[None, :] <= latent_offsets[:, None]
    cross_ctx = attention(latent_queries, hist_keys, hist_values, allowed)
    latent_mid = (latent_embed.astype(jnp.float32) + grouped_product(cross_ctx, w_out)).astype(jnp.bfloat16)
    widened = latent_mid.astype(jnp.float32)
    mean_square = lax.optimization_barrier(jnp.mean(widened * widened, axis=1, keepdims=True))
    normed = (widened * lax.rsqrt(mean_square + 1e-05) * norm_gain.astype(jnp.float32)).astype(jnp.bfloat16)
    self_queries = jnp.dot(normed, w_self_query, preferred_element_type=jnp.float32).astype(jnp.bfloat16)
    self_keys = jnp.dot(normed, w_self_key, preferred_element_type=jnp.float32).astype(jnp.bfloat16)
    self_values = jnp.dot(normed, w_self_value, preferred_element_type=jnp.float32).astype(jnp.bfloat16)
    latent_index = jnp.arange(Q, dtype=jnp.int32)
    causal = latent_index[None, :] <= latent_index[:, None]
    self_ctx = attention(self_queries, self_keys, self_values, causal)
    return (latent_mid.astype(jnp.float32) + grouped_product(self_ctx, w_self_out)).astype(jnp.bfloat16)
```

```python
import math

import jax
import jax.numpy as jnp
from jax import lax
from jax.sharding import PartitionSpec as P

HEAD_DIM = 128


def empty_state(row_count, head_count):
    return (
        jnp.full((head_count, row_count), -1e30, jnp.float32),
        jnp.zeros((head_count, row_count), jnp.float32),
        jnp.zeros((head_count, row_count, HEAD_DIM), jnp.float32),
    )


def attend_block(running, queries, limits, key_block, value_block, head_count):
    row_maxes, totals, weighted = running
    row_count = queries.shape[0]
    key_count = key_block.shape[0]
    query_heads = queries.reshape(row_count, head_count, HEAD_DIM)
    key_heads = key_block.reshape(key_count, head_count, HEAD_DIM)
    value_heads = value_block.reshape(key_count, head_count, HEAD_DIM)
    scores = jnp.einsum(
        "qhd,khd->hqk", query_heads, key_heads, preferred_element_type=jnp.float32
    ) * (1.0 / math.sqrt(HEAD_DIM))
    key_positions = jnp.arange(key_count, dtype=jnp.int32)
    allowed = key_positions[None, None, :] <= limits[None, :, None]
    scores = jnp.where(allowed, scores, -1e30)
    new_max = jnp.maximum(row_maxes, jnp.max(scores, axis=2))
    weights = jnp.where(allowed, jnp.exp(scores - new_max[:, :, None]), 0.0)
    totals = jnp.sum(weights, axis=2)
    weighted = jnp.einsum(
        "hqk,khd->hqd",
        weights.astype(jnp.bfloat16),
        value_heads,
        preferred_element_type=jnp.float32,
    )
    return (new_max, totals, weighted)


def finish(running):
    row_maxes, totals, weighted = running
    head_count, row_count = totals.shape
    context = weighted / totals[:, :, None]
    return context.transpose(1, 0, 2).reshape(row_count, head_count * HEAD_DIM).astype(jnp.bfloat16)


def per_device(
    history_ids,
    latent_offsets,
    byte_table,
    w_query,
    w_key,
    w_value,
    w_out,
    norm_gain,
    w_self_query,
    w_self_key,
    w_self_value,
    w_self_out,
):
    hist_index = lax.axis_index("hist")
    mp_index = lax.axis_index("mp")
    local_tokens = history_ids.shape[0]
    latent_count = latent_offsets.shape[0]
    share_width = w_key.shape[1]
    head_count = share_width // HEAD_DIM
    all_ids = lax.all_gather(history_ids, "hist", axis=0, tiled=True)
    vocab = byte_table.shape[0]
    vocab_ids = jnp.arange(vocab, dtype=jnp.int32)
    token_hot = (all_ids[:, None] == vocab_ids[None, :]).astype(jnp.bfloat16)
    places = jnp.arange(all_ids.shape[0], dtype=jnp.int32)
    seen = (places[None, :] <= latent_offsets[:, None]).astype(jnp.bfloat16)
    here = (places[None, :] == latent_offsets[:, None]).astype(jnp.bfloat16)
    counts = jnp.dot(seen, token_hot, preferred_element_type=jnp.float32)
    latent_hot = jnp.dot(here, token_hot, preferred_element_type=jnp.float32).astype(jnp.bfloat16)
    key_table, value_table = (
        jnp.dot(byte_table, w, preferred_element_type=jnp.float32).astype(jnp.bfloat16)
        for w in (w_key, w_value)
    )
    latent_embed = jnp.dot(latent_hot, byte_table, preferred_element_type=jnp.float32).astype(
        jnp.bfloat16
    )
    latent_queries = jnp.dot(latent_embed, w_query, preferred_element_type=jnp.float32).astype(
        jnp.bfloat16
    )
    query_heads = latent_queries.reshape(latent_count, head_count, HEAD_DIM)
    key_heads = key_table.reshape(vocab, head_count, HEAD_DIM)
    value_heads = value_table.reshape(vocab, head_count, HEAD_DIM)
    scores = jnp.einsum(
        "qhd,khd->hqk", query_heads, key_heads, preferred_element_type=jnp.float32
    ) * (1.0 / math.sqrt(HEAD_DIM))
    present = counts[None] > 0.0
    scores = jnp.where(present, scores, -1e30)
    row_maxes = jnp.max(scores, axis=2, keepdims=True)
    weights = jnp.where(present, jnp.exp(scores - row_maxes), 0.0) * counts[None]
    totals = jnp.sum(weights, axis=2)
    weighted = jnp.einsum(
        "hqk,khd->hqd",
        weights.astype(jnp.bfloat16),
        value_heads,
        preferred_element_type=jnp.float32,
    )
    cross_ctx = finish((None, totals, weighted))
    partial_value = jnp.dot(cross_ctx, w_out, preferred_element_type=jnp.float32)
    shared_part = lax.psum_scatter(
        partial_value.astype(jnp.bfloat16), "mp", scatter_dimension=1, tiled=True
    ).astype(jnp.float32)
    embed_slice = lax.dynamic_slice_in_dim(latent_embed, mp_index * share_width, share_width, 1)
    latent_part = (embed_slice.astype(jnp.float32) + shared_part).astype(jnp.bfloat16)
    latent_full = lax.all_gather(latent_part, "mp", axis=1, tiled=True)
    widened = latent_full.astype(jnp.float32)
    mean_square = jnp.mean(widened * widened, axis=1, keepdims=True)
    normed = (widened * lax.rsqrt(mean_square + 1e-05) * norm_gain.astype(jnp.float32)).astype(
        jnp.bfloat16
    )
    pieces = (
        lax.all_gather(w_self_query, "hist", axis=0, tiled=True),
        lax.all_gather(w_self_key, "hist", axis=0, tiled=True),
        lax.all_gather(w_self_value, "hist", axis=0, tiled=True),
    )
    self_q32, self_k32, self_v32 = tuple(
        (jnp.dot(normed, piece, preferred_element_type=jnp.float32) for piece in pieces)
    )
    self_queries = self_q32.astype(jnp.bfloat16)
    self_keys = self_k32.astype(jnp.bfloat16)
    self_values = self_v32.astype(jnp.bfloat16)
    latent_limits = hist_index * latent_count + jnp.arange(latent_count, dtype=jnp.int32)
    pieces = (
        lax.all_gather(self_keys, "hist", axis=0, tiled=True),
        lax.all_gather(self_values, "hist", axis=0, tiled=True),
    )
    self_state = attend_block(
        empty_state(latent_count, head_count),
        self_queries,
        latent_limits,
        pieces[0],
        pieces[1],
        head_count,
    )
    self_ctx = finish(self_state)
    out_terms = jnp.dot(
        self_ctx,
        lax.all_gather(w_self_out, "hist", axis=1, tiled=True),
        preferred_element_type=jnp.float32,
    )
    self_part = lax.psum_scatter(
        out_terms.astype(jnp.bfloat16), "mp", scatter_dimension=1, tiled=True
    ).astype(jnp.float32)
    return (latent_part.astype(jnp.float32) + self_part).astype(jnp.bfloat16)


def solution(mesh):
    return jax.shard_map(
        per_device,
        mesh=mesh,
        in_specs=(
            P("hist"),
            P("hist"),
            P(),
            P(None, "mp"),
            P(None, "mp"),
            P(None, "mp"),
            P("mp", None),
            P(),
            P("hist", "mp"),
            P("hist", "mp"),
            P("hist", "mp"),
            P("mp", "hist"),
        ),
        out_specs=P("hist", "mp"),
        check_vma=False,
    )
```

```python
import functools
import math

import jax
import jax.numpy as jnp
from jax import lax
from jax.experimental import pallas as pl
from jax.experimental.pallas import tpu as pltpu
from jax.sharding import PartitionSpec as P

HEAD_DIM = 128
MESH = pl.DeviceIdType.MESH
BF16 = jnp.bfloat16
F32 = jnp.float32
SCALE = 1.0 / math.sqrt(HEAD_DIM)
ROWS = 64
WIDE = 256
TOKENS = 512
NT = (((1,), (1,)), ((), ()))


def dot(a, b):
    return jnp.dot(a, b, preferred_element_type=F32)


def dot_nt(a, b):
    return lax.dot_general(a, b, NT, preferred_element_type=F32)


def kernel(
    small_ref, tab_hbm, wq_hbm, wk_hbm, wv_hbm, wo_hbm, wsq_hbm, wsk_hbm, wsv_hbm, wso_hbm,
    out_ref,
    ids, tab, wq, wk, wv, wo, wself, wso, ktab, qtab, vtab, acc, lat_hot,
    send1, recv1, mid, left, zsend, zrecv, ss_send, ss_recv, kv, queries, ctx, send2, recv2, resid,
    loc_sem, ids_s, ids_r, wself_s, wself_r, wso_s, wso_r, rs1_s, rs1_r, ag_s, ag_r,
    zx_s, zx_r, kv_s, kv_r, rs2_s, rs2_r, res_s, res_r,
):
    h = lax.axis_index("hist")
    m = lax.axis_index("mp")
    y, zh, c = h // 4, (h // 2) % 2, h % 2
    x, zl = m // 4, m % 4
    place = y * 2 + c

    def half_of(target_zl):
        own_pair = (target_zl // 2) == (zl // 2)
        inner = (zl == 1) | (zl == 2)
        return jnp.where(own_pair | inner, zh, 1 - zh)

    def peer(t):
        return (y * 4 + half_of(t % 4) * 2 + c, t)

    partner = (y * 4 + (1 - zh) * 2 + c, m)
    sibling = (y * 4 + zh * 2 + 1 - c, m)

    def y_peer(d):
        return (((y + d) % 4) * 4 + zh * 2 + c, m)

    def remote(src, dst, s, r, device):
        return pltpu.make_async_remote_copy(
            src_ref=src, dst_ref=dst, send_sem=s, recv_sem=r, device_id=device, device_id_type=MESH
        )

    def arrived(ref, sem):
        remote(ref, ref, sem, sem, partner).wait_recv()

    def left_here(ref, sem):
        remote(ref, ref, sem, sem, partner).wait_send()

    local = [
        pltpu.make_async_copy(small_ref.at[0:8], ids.at[h], loc_sem.at[0]),
        pltpu.make_async_copy(wsk_hbm, wself.at[place, 0], loc_sem.at[1]),
        pltpu.make_async_copy(wsv_hbm, wself.at[place, 1], loc_sem.at[2]),
        pltpu.make_async_copy(wsq_hbm, wself.at[place, 2], loc_sem.at[3]),
        pltpu.make_async_copy(wso_hbm, wso.at[h], loc_sem.at[4]),
        pltpu.make_async_copy(tab_hbm, tab, loc_sem.at[5]),
        pltpu.make_async_copy(wk_hbm, wk, loc_sem.at[6]),
        pltpu.make_async_copy(wv_hbm, wv, loc_sem.at[7]),
        pltpu.make_async_copy(wq_hbm, wq, loc_sem.at[8]),
    ]
    for b in range(8):
        column = ((b // 2) * 4 + half_of(b % 4) * 2 + (b % 2)) * WIDE
        local.append(
            pltpu.make_async_copy(
                wo_hbm.at[:, pl.ds(pl.multiple_of(column, WIDE), WIDE)], wo.at[b], loc_sem.at[9 + b]
            )
        )
    for copy in local:
        copy.start()

    barrier = pltpu.get_barrier_semaphore()

    @pl.loop(1, 32)
    def _(i):
        other = (zh * 16 + m + i) % 32
        device = (y * 4 + (other // 16) * 2 + c, other % 16)
        pl.semaphore_signal(barrier, inc=1, device_id=device, device_id_type=MESH)

    @pl.loop(1, 16)
    def _(i):
        pl.semaphore_signal(barrier, inc=1, device_id=((h + i) % 16, m), device_id_type=MESH)

    pl.semaphore_wait(barrier, 46)

    local[0].wait()

    @pl.loop(1, 16)
    def _(i):
        remote(ids.at[h], ids.at[h], ids_s.at[i], ids_r.at[h], ((h + i) % 16, m)).start()

    for copy in local[1:5]:
        copy.wait()
    for d in (1, 3, 2):
        remote(
            wself.at[place], wself.at[place], wself_s.at[d], wself_r.at[place], y_peer(d)
        ).start()
    remote(wself.at[place], wself.at[place], wself_s.at[0], wself_r.at[place], sibling).start()
    remote(wso.at[h], wso.at[h], wso_s.at[0], wso_r.at[h], partner).start()

    local[5].wait()
    local[6].wait()
    ktab[...] = dot(tab[...], wk[...]).astype(BF16)
    local[7].wait()
    vtab[...] = dot(tab[...], wv[...]).astype(BF16)
    local[8].wait()
    qtab[...] = dot(tab[...], wq[...]).astype(BF16)

    @pl.loop(1, 16)
    def _(i):
        b = (h + i) % 16
        arrived(ids.at[b], ids_r.at[b])

    offsets = ids[y * 4 + c][4:5, :] + ids[y * 4 + 2 + c][5:6, :]
    acc[...] = jnp.zeros_like(acc)
    vocab_iota = lax.broadcasted_iota(jnp.int32, (256, 128), 0).astype(F32)
    row_iota = lax.broadcasted_iota(jnp.int32, (128, 128), 0)

    @pl.loop(0, 16)
    def _(b):
        hots, masks = [], []
        for r in range(4):
            hots.append(jnp.where(vocab_iota == ids[b, r : r + 1, :], 1.0, 0.0).astype(BF16))
            places = (row_iota + (b * TOKENS + r * 128)).astype(F32)
            masks.append(
                jnp.concatenate(
                    [
                        jnp.where(places <= offsets, 1.0, 0.0).astype(BF16),
                        jnp.where(places == offsets, 1.0, 0.0).astype(BF16),
                    ],
                    axis=1,
                )
            )
        acc[...] += dot(jnp.concatenate(hots, axis=1), jnp.concatenate(masks, axis=0))

    counts = acc[:, :128].T
    hot = acc[:, 128:].T.astype(BF16)
    lat_hot[...] = hot
    latent_queries = dot(hot, qtab[...]).astype(BF16)
    present = counts > 0.0
    heads = []
    for hd in range(2):
        cols = slice(hd * HEAD_DIM, (hd + 1) * HEAD_DIM)
        scores = dot_nt(latent_queries[:, cols], ktab[:, cols]) * SCALE
        scores = jnp.where(present, scores, -1e30)
        top = jnp.max(scores, axis=1, keepdims=True)
        weights = jnp.where(present, jnp.exp(scores - top), 0.0) * counts
        total = jnp.sum(weights, axis=1, keepdims=True)
        heads.append(dot(weights.astype(BF16), vtab[:, cols]) / total)
    ctx[...] = jnp.concatenate(heads, axis=1).astype(BF16)

    for copy in local[9:]:
        copy.wait()

    @pl.loop(0, 8)
    def _(i):
        b = (m + i) % 8
        part = dot(ctx[...], wo[b]).astype(BF16)
        for r in range(2):
            t = r * 8 + b
            block = part[r * ROWS : (r + 1) * ROWS]
            send1[t] = block

            @pl.when(t == m)
            def _():
                recv1[m] = block

            @pl.when(t != m)
            def _():
                remote(send1.at[t], recv1.at[m], rs1_s.at[t], rs1_r.at[m], peer(t)).start()

    own_block = ((m % 8) // 2) * 4 + zh * 2 + m % 2
    total = dot(
        lat_hot[pl.ds(pl.multiple_of((m // 8) * ROWS, ROWS), ROWS)],
        tab[:, pl.ds(pl.multiple_of(own_block * WIDE, WIDE), WIDE)],
    )

    @pl.loop(1, 16)
    def _(i):
        s = (m + i) % 16
        arrived(recv1.at[s], rs1_r.at[s])

    sums = recv1[0].astype(F32)
    for s in range(1, 16):
        sums += recv1[s].astype(F32)
    mid[m] = (total + sums).astype(BF16)

    for d in range(1, 4):
        remote(
            mid.at[m], mid.at[m], ag_s.at[d], ag_r.at[m], (h, x * 4 + (zl + d) % 4)
        ).start()
    for d in (1, 3, 2):
        remote(
            mid.at[m], mid.at[m], ag_s.at[4 + d], ag_r.at[m], (h, ((x + d) % 4) * 4 + zl)
        ).start()
    for e in range(1, 4):
        t = x * 4 + (zl + e) % 4
        arrived(mid.at[t], ag_r.at[t])
        for d in (1, 3, 2):
            remote(
                mid.at[t], mid.at[t], ag_s.at[4 + e * 4 + d], ag_r.at[t], (h, ((x + d) % 4) * 4 + zl)
            ).start()

    for d in (1, 3, 2):
        slot = ((y + d) % 4) * 2 + c
        arrived(wself.at[slot], wself_r.at[slot])
        remote(
            wself.at[slot], wself.at[slot], wself_s.at[4 + d], wself_r.at[slot], sibling
        ).start()
    far = y * 4 + (1 - zh) * 2 + c
    arrived(wso.at[far], wso_r.at[far])
    for d in (1, 3, 2):
        remote(wso.at[h], wso.at[h], wso_s.at[d], wso_r.at[h], y_peer(d)).start()
        remote(wso.at[far], wso.at[far], wso_s.at[4 + d], wso_r.at[far], y_peer(d)).start()

    @pl.loop(4, 16)
    def _(i):
        t = (m - m % 4 + i) % 16
        arrived(mid.at[t], ag_r.at[t])

    squares = jnp.zeros((128, 128), F32)
    for b in range(8):
        rows = jnp.concatenate([mid[b], mid[8 + b]], axis=0).astype(F32)
        squares += rows[:, :128] * rows[:, :128] + rows[:, 128:] * rows[:, 128:]
        gain_row = 8 + ((b // 2) * 4 + zh * 2 + b % 2) * 2
        gain = jnp.concatenate(
            [small_ref[pl.ds(gain_row, 1), :], small_ref[pl.ds(gain_row + 1, 1), :]], axis=1
        )
        left[b] = (rows * gain).astype(BF16)
    square = jnp.broadcast_to(jnp.sum(squares, axis=1, keepdims=True), (128, 128)).T
    ss_send[...] = square[0:8]
    remote(ss_send, ss_recv, zx_s.at[3], zx_r.at[3], partner).start()

    for d in range(4):
        slot = d * 2 + 1 - c
        arrived(wself.at[slot], wself_r.at[slot])
    parts = []
    for j in range(3):
        part = dot(left[0], wself[0, j])
        for b in range(1, 8):
            part += dot(left[b], wself[b, j])
        parts.append(part)
        zsend[j] = part.astype(BF16)
        remote(zsend.at[j], zrecv.at[j], zx_s.at[j], zx_r.at[j], partner).start()

    own_bit = (m // 2) % 2
    home = (m // 4) * 2 + m % 2

    @pl.when(own_bit == zh)
    def _():
        away = (1 - zh) * 8 + home
        remote(mid.at[away], resid, res_s.at[0], res_r.at[0], partner).start()
        resid[...] = mid[zh * 8 + home]

    arrived(ss_recv, zx_r.at[3])
    square = ss_send[0:1] + ss_recv[0:1]
    norm = lax.rsqrt(square * (1.0 / 4096.0) + 1e-05)
    norm = jnp.broadcast_to(norm, (128, 128)).T
    norm = jnp.concatenate([norm, norm], axis=1)

    own_rows = pl.ds(pl.multiple_of(place * 128, 128), 128)
    for j in range(2):
        arrived(zrecv.at[j], zx_r.at[j])
        kv[j, own_rows, :] = ((parts[j] + zrecv[j].astype(F32)) * norm).astype(BF16)
        block = kv.at[j, own_rows, :]
        for d in (1, 3, 2):
            remote(block, block, kv_s.at[j * 8 + d], kv_r.at[j * 8 + place], y_peer(d)).start()
        remote(block, block, kv_s.at[j * 8], kv_r.at[j * 8 + place], sibling).start()
    arrived(zrecv.at[2], zx_r.at[2])
    queries[...] = ((parts[2] + zrecv[2].astype(F32)) * norm).astype(BF16)

    def kv_block(j, slot):
        return kv.at[j, pl.ds(pl.multiple_of(slot * 128, 128), 128), :]

    for j in range(2):
        for d in (1, 3, 2):
            slot = ((y + d) % 4) * 2 + c
            block = kv_block(j, slot)
            arrived(block, kv_r.at[j * 8 + slot])
            remote(block, block, kv_s.at[j * 8 + 4 + d], kv_r.at[j * 8 + slot], sibling).start()

    for d in (1, 3, 2):
        for half in range(2):
            slot = ((y + d) % 4) * 4 + half * 2 + c
            arrived(wso.at[slot], wso_r.at[slot])
    for d in range(4):
        for half in range(2):
            slot = d * 4 + half * 2 + c
            remote(
                wso.at[slot], wso.at[slot], wso_s.at[8 + d * 2 + half], wso_r.at[slot], sibling
            ).start()

    for j in range(2):
        for d in range(4):
            slot = d * 2 + 1 - c
            arrived(kv_block(j, slot), kv_r.at[j * 8 + slot])

    key_lane = lax.broadcasted_iota(jnp.int32, (128, 1024), 1)
    key_in = key_lane % 128
    key_place = (
        (key_lane // 256) * 256 + ((key_lane // 128) % 2) * 64 + (key_in // 64) * 128 + key_in % 64
    )
    query_row = lax.broadcasted_iota(jnp.int32, (128, 1024), 0)
    query_place = y * 256 + c * 64 + (query_row // 64) * 128 + query_row % 64
    allowed = key_place <= query_place
    heads = []
    for hd in range(2):
        cols = slice(hd * HEAD_DIM, (hd + 1) * HEAD_DIM)
        scores = dot_nt(queries[:, cols], kv[0, :, cols]) * SCALE
        scores = jnp.where(allowed, scores, -1e30)
        top = jnp.max(scores, axis=1, keepdims=True)
        weights = jnp.where(allowed, jnp.exp(scores - top), 0.0)
        total = jnp.sum(weights, axis=1, keepdims=True)
        heads.append(dot(weights.astype(BF16), kv[1, :, cols]) / total)
    ctx[...] = jnp.concatenate(heads, axis=1).astype(BF16)

    for d in range(4):
        for half in range(2):
            slot = d * 4 + half * 2 + 1 - c
            arrived(wso.at[slot], wso_r.at[slot])

    @pl.loop(0, 16)
    def _(i):
        t = (m + i) % 16
        rows = pl.ds(pl.multiple_of(half_of(t % 4) * ROWS, ROWS), ROWS)
        send2[t] = dot(ctx[rows, :], wso[t]).astype(BF16)

        @pl.when(t == m)
        def _():
            recv2[m] = send2[m]

        @pl.when(t != m)
        def _():
            remote(send2.at[t], recv2.at[m], rs2_s.at[t], rs2_r.at[m], peer(t)).start()

    @pl.when(own_bit != zh)
    def _():
        arrived(resid, res_r.at[0])

    @pl.loop(1, 16)
    def _(i):
        s = (m + i) % 16
        arrived(recv2.at[s], rs2_r.at[s])

    sums = resid[...].astype(F32)
    for s in range(16):
        sums += recv2[s].astype(F32)
    out_ref[...] = sums.astype(BF16)

    @pl.loop(1, 16)
    def _(i):
        left_here(ids.at[h], ids_s.at[i])
        s = (m + i) % 16
        left_here(send1.at[s], rs1_s.at[s])
        left_here(send2.at[s], rs2_s.at[s])

    @pl.loop(0, 8)
    def _(i):
        @pl.when(i != 4)
        def _():
            left_here(wself.at[0], wself_s.at[i])
            left_here(kv_block(0, 0), kv_s.at[i])
            left_here(kv_block(0, 0), kv_s.at[8 + i])

    @pl.loop(0, 16)
    def _(i):
        @pl.when(i != 4)
        def _():
            left_here(wso.at[0], wso_s.at[i])

    for i in (1, 2, 3, 5, 6, 7, 9, 10, 11, 13, 14, 15, 17, 18, 19):
        left_here(mid.at[0], ag_s.at[i])
    for j in range(3):
        left_here(zsend.at[j], zx_s.at[j])
    left_here(ss_send, zx_s.at[3])

    @pl.when(own_bit == zh)
    def _():
        left_here(resid, res_s.at[0])


def per_device(
    history_ids, latent_offsets, byte_table, w_query, w_key, w_value, w_out, norm_gain,
    w_self_query, w_self_key, w_self_value, w_self_out,
):
    offsets = latent_offsets.astype(F32)
    small = jnp.concatenate(
        [
            history_ids.astype(F32),
            offsets,
            jnp.zeros((128,), F32),
            offsets,
            jnp.zeros((256,), F32),
            norm_gain.astype(F32),
        ]
    ).reshape(40, 128)
    vmem = pl.BlockSpec(memory_space=pltpu.VMEM)
    hbm = pl.BlockSpec(memory_space=pl.ANY)
    dma = pltpu.SemaphoreType.DMA
    scratch = [
        pltpu.VMEM((16, 8, 128), F32),
        pltpu.VMEM((256, 4096), BF16),
        pltpu.VMEM((4096, 256), BF16),
        pltpu.VMEM((4096, 256), BF16),
        pltpu.VMEM((4096, 256), BF16),
        pltpu.VMEM((8, 256, 256), BF16),
        pltpu.VMEM((8, 3, 256, 256), BF16),
        pltpu.VMEM((16, 256, 256), BF16),
        pltpu.VMEM((256, 256), BF16),
        pltpu.VMEM((256, 256), BF16),
        pltpu.VMEM((256, 256), BF16),
        pltpu.VMEM((256, 256), F32),
        pltpu.VMEM((128, 256), BF16),
        pltpu.VMEM((16, ROWS, WIDE), BF16),
        pltpu.VMEM((16, ROWS, WIDE), BF16),
        pltpu.VMEM((16, ROWS, WIDE), BF16),
        pltpu.VMEM((8, 128, WIDE), BF16),
        pltpu.VMEM((3, 128, WIDE), BF16),
        pltpu.VMEM((3, 128, WIDE), BF16),
        pltpu.VMEM((8, 128), F32),
        pltpu.VMEM((8, 128), F32),
        pltpu.VMEM((2, 1024, WIDE), BF16),
        pltpu.VMEM((128, WIDE), BF16),
        pltpu.VMEM((128, WIDE), BF16),
        pltpu.VMEM((16, ROWS, WIDE), BF16),
        pltpu.VMEM((16, ROWS, WIDE), BF16),
        pltpu.VMEM((ROWS, WIDE), BF16),
    ] + [dma((n,)) for n in (17, 16, 16, 8, 8, 16, 16, 16, 16, 20, 16, 4, 4, 16, 16, 16, 16, 1, 1)]
    return pl.pallas_call(
        kernel,
        out_shape=jax.ShapeDtypeStruct((ROWS, WIDE), BF16),
        in_specs=[vmem] + [hbm] * 9,
        out_specs=vmem,
        scratch_shapes=scratch,
        compiler_params=pltpu.CompilerParams(
            collective_id=0, has_side_effects=True, vmem_limit_bytes=56 * 1024 * 1024
        ),
        cost_estimate=pl.CostEstimate(
            flops=5_000_000_000, bytes_accessed=12_000_000, transcendentals=400_000
        ),
    )(
        small, byte_table, w_query, w_key, w_value, w_out,
        w_self_query, w_self_key, w_self_value, w_self_out,
    )


def solution(mesh):
    return jax.shard_map(
        per_device,
        mesh=mesh,
        in_specs=(
            P("hist"),
            P("hist"),
            P(),
            P(None, "mp"),
            P(None, "mp"),
            P(None, "mp"),
            P("mp", None),
            P(),
            P("hist", "mp"),
            P("hist", "mp"),
            P("hist", "mp"),
            P("mp", "hist"),
        ),
        out_specs=P("hist", "mp"),
        check_vma=False,
    )
```

```python
import functools
import math

import jax
import jax.numpy as jnp
from jax import lax
from jax.experimental import pallas as pl
from jax.experimental.pallas import tpu as pltpu
from jax.sharding import PartitionSpec as P

HEAD_DIM = 128
MESH = pl.DeviceIdType.MESH
BF16 = jnp.bfloat16
F32 = jnp.float32
SCALE = 1.0 / math.sqrt(HEAD_DIM)
ROWS = 64
WIDE = 256
TOKENS = 512
NT = (((1,), (1,)), ((), ()))


def dot(a, b):
    return jnp.dot(a, b, preferred_element_type=F32)


def dot_nt(a, b):
    return lax.dot_general(a, b, NT, preferred_element_type=F32)


def kernel(
    ids_hbm, offs_hbm, gain_hbm, tab_hbm, wq_hbm, wk_hbm, wv_hbm, wo_hbm,
    wsq_hbm, wsk_hbm, wsv_hbm, wso_hbm,
    out_ref,
    ids, offs, gains, gain_rows, tab, wq, wk, wv, wo, wself, wso, ktab, qtab, vtab, lat_hot,
    send1, recv1, mid, left, zsend, zrecv, ss_send, ss_recv, kv, queries, ctx, send2, recv2, resid,
    loc_sem, ids_s, ids_r, wself_s, wself_r, wso_s, wso_r, rs1_s, rs1_r, ag_s, ag_r,
    zx_s, zx_r, kv_s, kv_r, rs2_s, rs2_r, res_s, res_r, offs_s, offs_r,
):
    h = lax.axis_index("hist")
    m = lax.axis_index("mp")
    y, zh, c = h // 4, (h // 2) % 2, h % 2
    x, zl = m // 4, m % 4
    place = y * 2 + c
    at_edge = (zl == 0) | (zl == 3)
    nearest = jnp.where(zl < 2, 3, 0)
    served = jnp.where(zl == 0, 2, 0)

    def half_of(target_zl):
        own_pair = (target_zl // 2) == (zl // 2)
        inner = (zl == 1) | (zl == 2)
        return jnp.where(own_pair | inner, zh, 1 - zh)

    def peer(t):
        return (y * 4 + half_of(t % 4) * 2 + c, t)

    def source(t):
        return (y * 4 + jnp.where(t % 4 == nearest, 1 - zh, zh) * 2 + c, t)

    partner = (y * 4 + (1 - zh) * 2 + c, m)
    sibling = (y * 4 + zh * 2 + 1 - c, m)

    def same_z(i):
        other = (place + i) % 8
        return ((other // 2) * 4 + zh * 2 + other % 2, m)

    def y_peer(d):
        return (((y + d) % 4) * 4 + zh * 2 + c, m)

    def remote(src, dst, s, r, device):
        return pltpu.make_async_remote_copy(
            src_ref=src, dst_ref=dst, send_sem=s, recv_sem=r, device_id=device, device_id_type=MESH
        )

    def arrived(ref, sem):
        remote(ref, ref, sem, sem, partner).wait_recv()

    def left_here(ref, sem):
        remote(ref, ref, sem, sem, partner).wait_send()

    far = y * 4 + (1 - zh) * 2 + c

    def half_slot(slot, k):
        return wso.at[slot, pl.ds(k * 128, 128)]

    def cross_output_weights(k):
        part = half_slot(h, k)
        remote(part, part, wso_s.at[k], wso_r.at[16 + h * 2 + k], partner).start()

    def spread_far(k):
        part = half_slot(far, k)
        arrived(part, wso_r.at[16 + far * 2 + k])
        for d in (1, 3, 2):
            remote(
                part, part, wso_s.at[6 + k * 4 + d], wso_r.at[16 + far * 2 + k], y_peer(d)
            ).start()

    barrier = pltpu.get_barrier_semaphore()

    def greet(device):
        pl.semaphore_signal(barrier, inc=1, device_id=device, device_id_type=MESH)

    greet(partner)

    @pl.loop(0, 8)
    def _(i):
        greet(((i // 2) * 4 + (1 - zh) * 2 + i % 2, x * 4 + nearest))

    @pl.loop(1, 16)
    def _(i):
        t = (m + i) % 16
        greet(source(t))

    @pl.loop(1, 8)
    def _(i):
        greet(same_z(i))

    @pl.loop(1, 4)
    def _(i):
        greet((h, x * 4 + (zl + i) % 4))

    local = [
        pltpu.make_async_copy(ids_hbm, ids.at[h], loc_sem.at[0]),
        pltpu.make_async_copy(offs_hbm, offs.at[zh], loc_sem.at[17]),
        pltpu.make_async_copy(wsk_hbm, wself.at[place, 0], loc_sem.at[1]),
        pltpu.make_async_copy(wsv_hbm, wself.at[place, 1], loc_sem.at[2]),
        pltpu.make_async_copy(wsq_hbm, wself.at[place, 2], loc_sem.at[3]),
        pltpu.make_async_copy(wso_hbm, wso.at[h], loc_sem.at[4]),
        pltpu.make_async_copy(tab_hbm, tab, loc_sem.at[5]),
        pltpu.make_async_copy(wk_hbm, wk, loc_sem.at[6]),
        pltpu.make_async_copy(wv_hbm, wv, loc_sem.at[7]),
        pltpu.make_async_copy(wq_hbm, wq, loc_sem.at[8]),
        pltpu.make_async_copy(gain_hbm, gains, loc_sem.at[18]),
    ]
    for b in range(8):
        column = ((b // 2) * 4 + half_of(b % 4) * 2 + (b % 2)) * WIDE
        local.append(
            pltpu.make_async_copy(
                wo_hbm.at[:, pl.ds(pl.multiple_of(column, WIDE), WIDE)], wo.at[b], loc_sem.at[9 + b]
            )
        )
    for copy in local:
        copy.start()

    pl.semaphore_wait(barrier, 26 + jnp.where(at_edge, 16, 0))

    @pl.when(at_edge)
    def _():
        @pl.loop(0, 16)
        def _(i):
            device = (((i // 2) % 4) * 4 + (1 - zh) * 2 + i % 2, x * 4 + served + i // 8)
            remote(ids_hbm, ids.at[h], ids_s.at[8 + i], ids_r.at[h], device).start()

        for i in range(2):
            device = (y * 4 + (1 - zh) * 2 + c, x * 4 + served + i)
            remote(offs_hbm, offs.at[zh], offs_s.at[i], offs_r.at[0], device).start()

    @pl.loop(1, 8)
    def _(i):
        remote(ids_hbm, ids.at[h], ids_s.at[i], ids_r.at[h], same_z(i)).start()

    for copy in local[2:6]:
        copy.wait()
    for d in (1, 3, 2):
        remote(
            wself.at[place], wself.at[place], wself_s.at[d], wself_r.at[place], y_peer(d)
        ).start()
    remote(wself.at[place], wself.at[place], wself_s.at[0], wself_r.at[place], sibling).start()

    local[6].wait()
    local[7].wait()
    ktab[...] = dot(tab[...], wk[...]).astype(BF16)
    local[8].wait()
    vtab[...] = dot(tab[...], wv[...]).astype(BF16)
    local[9].wait()
    qtab[...] = dot(tab[...], wq[...]).astype(BF16)

    local[0].wait()
    local[1].wait()

    @pl.loop(1, 8)
    def _(i):
        other = (place + i) % 8
        b = (other // 2) * 4 + zh * 2 + other % 2
        arrived(ids.at[b], ids_r.at[b])

    vocab_iota = lax.broadcasted_iota(jnp.int32, (256, 128), 0)
    row_iota = lax.broadcasted_iota(jnp.int32, (128, 128), 0)

    def earlier(half, seen):
        def add(i, seen):
            b = (i // 2) * 4 + half * 2 + i % 2
            return sum(
                (jnp.where(vocab_iota == ids[b, r : r + 1, :], 1.0, 0.0) for r in range(4)), seen
            )

        return lax.fori_loop(0, y * 2, add, seen)

    def token_hot(b):
        return jnp.concatenate(
            [jnp.where(vocab_iota == ids[b, r : r + 1, :], 1.0, 0.0).astype(BF16) for r in range(4)],
            axis=1,
        )

    def masks(b, offsets):
        blocks = []
        for r in range(4):
            places = row_iota + (b * TOKENS + r * 128)
            blocks.append(
                jnp.concatenate(
                    [
                        jnp.where(places <= offsets, 1.0, 0.0).astype(BF16),
                        jnp.where(places == offsets, 1.0, 0.0).astype(BF16),
                    ],
                    axis=1,
                )
            )
        return jnp.concatenate(blocks, axis=0)

    seen = earlier(zh, jnp.zeros((256, 128), F32))
    near_hots = [token_hot(y * 4 + zh * 2 + q) for q in range(2)]

    @pl.loop(0, 8)
    def _(i):
        b = (i // 2) * 4 + (1 - zh) * 2 + i % 2
        arrived(ids.at[b], ids_r.at[b])

    arrived(offs.at[1 - zh], offs_r.at[0])

    cross_output_weights(0)

    offsets = jnp.concatenate([offs[0], offs[1]], axis=1)
    counted = jnp.zeros((256, 256), F32)
    for q in range(2):
        counted += dot(near_hots[q], masks(y * 4 + zh * 2 + q, offsets))
        b = y * 4 + (1 - zh) * 2 + q
        counted += dot(token_hot(b), masks(b, offsets))
    seen = earlier(1 - zh, seen)

    counts = (counted[:, :128] + jnp.sum(seen, axis=1, keepdims=True)).T
    hot = counted[:, 128:].T.astype(BF16)
    lat_hot[...] = hot
    latent_queries = dot(hot, qtab[...]).astype(BF16)
    present = counts > 0.0
    heads = []
    for hd in range(2):
        cols = slice(hd * HEAD_DIM, (hd + 1) * HEAD_DIM)
        scores = dot_nt(latent_queries[:, cols], ktab[:, cols]) * SCALE
        scores = jnp.where(present, scores, -1e30)
        top = jnp.max(scores, axis=1, keepdims=True)
        weights = jnp.where(present, jnp.exp(scores - top), 0.0) * counts
        total = jnp.sum(weights, axis=1, keepdims=True)
        heads.append(dot(weights.astype(BF16), vtab[:, cols]) / total)
    ctx[...] = jnp.concatenate(heads, axis=1).astype(BF16)

    for copy in local[11:]:
        copy.wait()
    turn = 3 - 2 * (zl % 2)
    z_order = [(zl + e) % 4 for e in (2, turn, 4 - turn, 0)]
    for other in z_order:
        for e in range(2):
            b = ((x + e) % 2) * 4 + other
            part = dot(ctx[...], wo[b]).astype(BF16)
            send1[b] = part[:ROWS]
            send1[8 + b] = part[ROWS:]
            for d in (1, 3) if e else (2, 0):
                t = ((x + d) % 4) * 4 + other

                def send(t=t):
                    remote(send1.at[t], recv1.at[m], rs1_s.at[t], rs1_r.at[m], peer(t)).start()

                if d or other is not z_order[3]:
                    send()
    recv1[m] = send1[m]

    own_block = ((m % 8) // 2) * 4 + zh * 2 + m % 2
    total = dot(
        lat_hot[pl.ds(pl.multiple_of((m // 8) * ROWS, ROWS), ROWS)],
        tab[:, pl.ds(pl.multiple_of(own_block * WIDE, WIDE), WIDE)],
    )

    @pl.loop(1, 16)
    def _(i):
        s = (m + i) % 16
        arrived(recv1.at[s], rs1_r.at[s])

    sums = recv1[0].astype(F32)
    for s in range(1, 16):
        sums += recv1[s].astype(F32)
    mid[m] = (total + sums).astype(BF16)

    order = (zl + 1 - 2 * (zl % 2), jnp.where(zl < 2, 2, 1), jnp.where(zl < 2, 3, 0))
    for e, other in enumerate(order):
        remote(
            mid.at[m], mid.at[m], ag_s.at[1 + e], ag_r.at[m], (h, x * 4 + other)
        ).start()
    for d in (1, 3, 2):
        remote(
            mid.at[m], mid.at[m], ag_s.at[4 + d], ag_r.at[m], (h, ((x + d) % 4) * 4 + zl)
        ).start()
    for d in (1, 3, 2):
        remote(wso.at[h], wso.at[h], wso_s.at[2 + d], wso_r.at[h], y_peer(d)).start()
    spread_far(0)

    for e, other in enumerate(order):
        t = x * 4 + other
        arrived(mid.at[t], ag_r.at[t])
        for d in (1, 3, 2):
            remote(
                mid.at[t], mid.at[t], ag_s.at[8 + e * 4 + d], ag_r.at[t], (h, ((x + d) % 4) * 4 + zl)
            ).start()

    cross_output_weights(1)

    for d in (1, 3, 2):
        slot = ((y + d) % 4) * 2 + c
        arrived(wself.at[slot], wself_r.at[slot])
        remote(
            wself.at[slot], wself.at[slot], wself_s.at[4 + d], wself_r.at[slot], sibling
        ).start()

    local[10].wait()
    gain_rows[...] = gains[...].astype(F32)

    @pl.loop(4, 16)
    def _(i):
        t = (m - m % 4 + i) % 16
        arrived(mid.at[t], ag_r.at[t])

    squares = jnp.zeros((128, 128), F32)
    for b in range(8):
        rows = jnp.concatenate([mid[b], mid[8 + b]], axis=0).astype(F32)
        squares += rows[:, :128] * rows[:, :128] + rows[:, 128:] * rows[:, 128:]
        first = ((b // 2) * 4 + zh * 2 + b % 2) * 2
        gain = [gain_rows[pl.ds(first + i, 1), :] for i in range(2)]
        left[b] = (rows * jnp.concatenate(gain, axis=1)).astype(BF16)

    for d in range(4):
        slot = d * 2 + 1 - c
        arrived(wself.at[slot], wself_r.at[slot])

    def project(j):
        part = dot(left[0], wself[0, j])
        for b in range(1, 8):
            part += dot(left[b], wself[b, j])
        zsend[j, 0] = part[:ROWS].astype(BF16)
        zsend[j, 1] = part[ROWS:].astype(BF16)
        return part

    def push(j):
        for r in range(2):
            k = j * 2 + r
            remote(zsend.at[j, r], zrecv.at[j, r], zx_s.at[k], zx_r.at[k], partner).start()

    def pushed(j):
        for r in range(2):
            left_here(zsend.at[j, r], zx_s.at[j * 2 + r])

    parts = [project(0)]
    push(0)
    square = jnp.broadcast_to(jnp.sum(squares, axis=1, keepdims=True), (128, 128)).T
    ss_send[...] = square[0:8]
    remote(ss_send, ss_recv, zx_s.at[6], zx_r.at[6], partner).start()
    parts.append(project(1))
    pushed(0)
    push(1)
    parts.append(project(2))
    pushed(1)
    push(2)

    own_bit = (m // 2) % 2
    home = (m // 4) * 2 + m % 2

    @pl.when(own_bit == zh)
    def _():
        away = (1 - zh) * 8 + home
        remote(mid.at[away], resid, res_s.at[0], res_r.at[0], partner).start()
        resid[...] = mid[zh * 8 + home]

    spread_far(1)

    arrived(ss_recv, zx_r.at[6])
    square = ss_send[0:1] + ss_recv[0:1]
    norm = lax.rsqrt(square * (1.0 / 4096.0) + 1e-05)
    norm = jnp.broadcast_to(norm, (128, 128)).T
    norm = jnp.concatenate([norm, norm], axis=1)

    for d in (1, 3, 2):
        slot = ((y + d) % 4) * 4 + zh * 2 + c
        arrived(wso.at[slot], wso_r.at[slot])
    for d in range(4):
        slot = d * 4 + zh * 2 + c
        remote(wso.at[slot], wso.at[slot], wso_s.at[16 + d], wso_r.at[slot], sibling).start()

    def kv_block(j, slot, r):
        return kv.at[j, pl.ds(pl.multiple_of(slot * 128 + r * ROWS, ROWS), ROWS), :]

    def whole(j, r):
        arrived(zrecv.at[j, r], zx_r.at[j * 2 + r])
        rows = slice(r * ROWS, (r + 1) * ROWS)
        return ((parts[j][rows] + zrecv[j, r].astype(F32)) * norm[rows]).astype(BF16)

    for j in range(2):
        for r in range(2):
            block = kv_block(j, place, r)
            block[...] = whole(j, r)
            k = (j * 2 + r) * 8
            for d in (1, 3, 2):
                remote(block, block, kv_s.at[k + d], kv_r.at[k + place], y_peer(d)).start()
            remote(block, block, kv_s.at[k], kv_r.at[k + place], sibling).start()

    def pass_block(j, r):
        k = (j * 2 + r) * 8
        for d in (1, 3, 2):
            slot = ((y + d) % 4) * 2 + c
            block = kv_block(j, slot, r)
            arrived(block, kv_r.at[k + slot])
            remote(block, block, kv_s.at[k + 4 + d], kv_r.at[k + slot], sibling).start()

    def wait_block(j, r):
        for d in range(4):
            slot = d * 2 + 1 - c
            arrived(kv_block(j, slot, r), kv_r.at[(j * 2 + r) * 8 + slot])

    pass_block(0, 0)
    pass_block(0, 1)
    queries[0:ROWS] = whole(2, 0)
    queries[ROWS:] = whole(2, 1)

    for d in (1, 3, 2):
        slot = ((y + d) % 4) * 4 + (1 - zh) * 2 + c
        for k in range(2):
            arrived(half_slot(slot, k), wso_r.at[16 + slot * 2 + k])
    for d in range(4):
        slot = d * 4 + (1 - zh) * 2 + c
        remote(wso.at[slot], wso.at[slot], wso_s.at[20 + d], wso_r.at[slot], sibling).start()

    wait_block(0, 0)
    wait_block(0, 1)

    key_lane = lax.broadcasted_iota(jnp.int32, (128, 1024), 1)
    key_in = key_lane % 128
    key_place = (
        (key_lane // 256) * 256 + ((key_lane // 128) % 2) * 64 + (key_in // 64) * 128 + key_in % 64
    )
    query_row = lax.broadcasted_iota(jnp.int32, (128, 1024), 0)
    query_place = y * 256 + c * 64 + (query_row // 64) * 128 + query_row % 64
    allowed = key_place <= query_place
    spread, totals = [], []
    for hd in range(2):
        cols = slice(hd * HEAD_DIM, (hd + 1) * HEAD_DIM)
        scores = dot_nt(queries[:, cols], kv[0, :, cols]) * SCALE
        scores = jnp.where(allowed, scores, -1e30)
        top = jnp.max(scores, axis=1, keepdims=True)
        weights = jnp.where(allowed, jnp.exp(scores - top), 0.0)
        totals.append(jnp.sum(weights, axis=1, keepdims=True))
        spread.append(weights.astype(BF16))

    pass_block(1, 0)
    pass_block(1, 1)

    wait_block(1, 0)
    wait_block(1, 1)

    heads = []
    for hd in range(2):
        cols = slice(hd * HEAD_DIM, (hd + 1) * HEAD_DIM)
        heads.append(dot(spread[hd], kv[1, :, cols]) / totals[hd])
    ctx[...] = jnp.concatenate(heads, axis=1).astype(BF16)

    for d in range(4):
        for half in range(2):
            slot = d * 4 + half * 2 + 1 - c
            arrived(wso.at[slot], wso_r.at[slot])

    def self_part(t):
        rows = pl.ds(pl.multiple_of(half_of(t % 4) * ROWS, ROWS), ROWS)
        return dot(ctx[rows, :], wso[t]).astype(BF16)

    for other in z_order:
        for d in (2, 1, 3, 0):
            t = ((x + d) % 4) * 4 + other
            if d or other is not z_order[3]:
                send2[t] = self_part(t)
                remote(send2.at[t], recv2.at[m], rs2_s.at[t], rs2_r.at[m], peer(t)).start()
    recv2[m] = self_part(m)

    @pl.when(own_bit != zh)
    def _():
        arrived(resid, res_r.at[0])

    @pl.loop(1, 16)
    def _(i):
        s = (m + i) % 16
        arrived(recv2.at[s], rs2_r.at[s])

    sums = resid[...].astype(F32)
    for s in range(16):
        sums += recv2[s].astype(F32)
    out_ref[...] = sums.astype(BF16)

    @pl.loop(1, 16)
    def _(i):
        s = (m + i) % 16
        left_here(send1.at[s], rs1_s.at[s])
        left_here(send2.at[s], rs2_s.at[s])

    @pl.when(at_edge)
    def _():
        @pl.loop(0, 16)
        def _(i):
            left_here(ids.at[h], ids_s.at[8 + i])

        for i in range(2):
            left_here(offs.at[0], offs_s.at[i])

    @pl.loop(1, 8)
    def _(i):
        left_here(ids.at[h], ids_s.at[i])

    @pl.loop(0, 8)
    def _(i):
        @pl.when(i != 4)
        def _():
            left_here(wself.at[0], wself_s.at[i])
            for k in range(4):
                left_here(kv_block(0, 0, 0), kv_s.at[k * 8 + i])

    for i in (0, 1, 7, 8, 9, 11, 12, 13):
        left_here(half_slot(0, 0), wso_s.at[i])
    for i in (3, 4, 5, 16, 17, 18, 19, 20, 21, 22, 23):
        left_here(wso.at[0], wso_s.at[i])

    for i in (1, 2, 3, 5, 6, 7, 9, 10, 11, 13, 14, 15, 17, 18, 19):
        left_here(mid.at[0], ag_s.at[i])
    pushed(2)
    left_here(ss_send, zx_s.at[6])

    @pl.when(own_bit == zh)
    def _():
        left_here(resid, res_s.at[0])


def per_device(
    history_ids, latent_offsets, byte_table, w_query, w_key, w_value, w_out, norm_gain,
    w_self_query, w_self_key, w_self_value, w_self_out,
):
    vmem = pl.BlockSpec(memory_space=pltpu.VMEM)
    hbm = pl.BlockSpec(memory_space=pl.ANY)
    dma = pltpu.SemaphoreType.DMA
    scratch = [
        pltpu.VMEM((16, 4, 128), jnp.int32),
        pltpu.VMEM((2, 1, 64), jnp.int32),
        pltpu.VMEM((32, 128), BF16),
        pltpu.VMEM((32, 128), F32),
        pltpu.VMEM((256, 4096), BF16),
        pltpu.VMEM((4096, 256), BF16),
        pltpu.VMEM((4096, 256), BF16),
        pltpu.VMEM((4096, 256), BF16),
        pltpu.VMEM((8, 256, 256), BF16),
        pltpu.VMEM((8, 3, 256, 256), BF16),
        pltpu.VMEM((16, 256, 256), BF16),
        pltpu.VMEM((256, 256), BF16),
        pltpu.VMEM((256, 256), BF16),
        pltpu.VMEM((256, 256), BF16),
        pltpu.VMEM((128, 256), BF16),
        pltpu.VMEM((16, ROWS, WIDE), BF16),
        pltpu.VMEM((16, ROWS, WIDE), BF16),
        pltpu.VMEM((16, ROWS, WIDE), BF16),
        pltpu.VMEM((8, 128, WIDE), BF16),
        pltpu.VMEM((3, 2, ROWS, WIDE), BF16),
        pltpu.VMEM((3, 2, ROWS, WIDE), BF16),
        pltpu.VMEM((8, 128), F32),
        pltpu.VMEM((8, 128), F32),
        pltpu.VMEM((2, 1024, WIDE), BF16),
        pltpu.VMEM((128, WIDE), BF16),
        pltpu.VMEM((128, WIDE), BF16),
        pltpu.VMEM((16, ROWS, WIDE), BF16),
        pltpu.VMEM((16, ROWS, WIDE), BF16),
        pltpu.VMEM((ROWS, WIDE), BF16),
    ] + [dma((n,)) for n in (
        19, 24, 16, 8, 8, 24, 48, 16, 16, 20, 16, 7, 7, 32, 32, 16, 16, 1, 1, 2, 1
    )]
    return pl.pallas_call(
        kernel,
        out_shape=jax.ShapeDtypeStruct((ROWS, WIDE), BF16),
        in_specs=[hbm] * 12,
        out_specs=vmem,
        scratch_shapes=scratch,
        compiler_params=pltpu.CompilerParams(
            collective_id=0, has_side_effects=True, vmem_limit_bytes=56 * 1024 * 1024
        ),
        cost_estimate=pl.CostEstimate(
            flops=5_000_000_000, bytes_accessed=12_000_000, transcendentals=400_000
        ),
    )(
        history_ids.reshape(4, 128), latent_offsets.reshape(1, 64), norm_gain.reshape(32, 128),
        byte_table, w_query, w_key, w_value, w_out,
        w_self_query, w_self_key, w_self_value, w_self_out,
    )


def solution(mesh):
    return jax.shard_map(
        per_device,
        mesh=mesh,
        in_specs=(
            P("hist"),
            P("hist"),
            P(),
            P(None, "mp"),
            P(None, "mp"),
            P(None, "mp"),
            P("mp", None),
            P(),
            P("hist", "mp"),
            P("hist", "mp"),
            P("hist", "mp"),
            P("mp", "hist"),
        ),
        out_specs=P("hist", "mp"),
        check_vma=False,
    )
```

```python
import functools
import math

import jax
import jax.numpy as jnp
from jax import lax
from jax.experimental import pallas as pl
from jax.experimental.pallas import tpu as pltpu
from jax.sharding import PartitionSpec as P

HEAD_DIM = 128
MESH = pl.DeviceIdType.MESH
BF16 = jnp.bfloat16
F32 = jnp.float32
SCALE = 1.0 / math.sqrt(HEAD_DIM)
ROWS = 64
WIDE = 256
TOKENS = 512
NT = (((1,), (1,)), ((), ()))


def dot(a, b):
    return jnp.dot(a, b, preferred_element_type=F32)


def dot_nt(a, b):
    return lax.dot_general(a, b, NT, preferred_element_type=F32)


def kernel(
    ids_hbm, offs_hbm, gain_hbm, tab_hbm, wq_hbm, wk_hbm, wv_hbm, wo_hbm,
    wsq_hbm, wsk_hbm, wsv_hbm, wso_hbm,
    out_ref,
    ids, offs, gains, gain_rows, tab, wq, wk, wv, wo, wself, wso, ktab, qtab, vtab, lat_hot,
    send1, recv1, mid, left, zsend, zrecv, ss_send, ss_recv, kv, queries, ctx, send2, recv2, resid,
    loc_sem, ids_s, ids_r, wself_s, wself_r, wso_s, wso_r, rs1_s, rs1_r, ag_s, ag_r,
    zx_s, zx_r, kv_s, kv_r, rs2_s, rs2_r, res_s, res_r, offs_s, offs_r,
):
    h = lax.axis_index("hist")
    m = lax.axis_index("mp")
    y, zh, c = h // 4, (h // 2) % 2, h % 2
    x, zl = m // 4, m % 4
    place = y * 2 + c
    at_edge = (zl == 0) | (zl == 3)
    nearest = jnp.where(zl < 2, 3, 0)
    served = jnp.where(zl == 0, 2, 0)

    def half_of(target_zl):
        own_pair = (target_zl // 2) == (zl // 2)
        inner = (zl == 1) | (zl == 2)
        return jnp.where(own_pair | inner, zh, 1 - zh)

    def peer(t):
        return (y * 4 + half_of(t % 4) * 2 + c, t)

    def source(t):
        return (y * 4 + jnp.where(t % 4 == nearest, 1 - zh, zh) * 2 + c, t)

    partner = (y * 4 + (1 - zh) * 2 + c, m)
    sibling = (y * 4 + zh * 2 + 1 - c, m)

    def same_z(i):
        other = (place + i) % 8
        return ((other // 2) * 4 + zh * 2 + other % 2, m)

    def y_peer(d):
        return (((y + d) % 4) * 4 + zh * 2 + c, m)

    def remote(src, dst, s, r, device):
        return pltpu.make_async_remote_copy(
            src_ref=src, dst_ref=dst, send_sem=s, recv_sem=r, device_id=device, device_id_type=MESH
        )

    def arrived(ref, sem):
        remote(ref, ref, sem, sem, partner).wait_recv()

    def left_here(ref, sem):
        remote(ref, ref, sem, sem, partner).wait_send()

    far = y * 4 + (1 - zh) * 2 + c

    def half_slot(slot, k):
        return wso.at[slot, pl.ds(k * 128, 128)]

    def cross_output_weights(k):
        part = half_slot(h, k)
        remote(part, part, wso_s.at[k], wso_r.at[16 + h * 2 + k], partner).start()

    def spread_far(k):
        part = half_slot(far, k)
        arrived(part, wso_r.at[16 + far * 2 + k])
        for d in (1, 3, 2):
            remote(
                part, part, wso_s.at[6 + k * 4 + d], wso_r.at[16 + far * 2 + k], y_peer(d)
            ).start()

    barrier = pltpu.get_barrier_semaphore()

    def greet(device):
        pl.semaphore_signal(barrier, inc=1, device_id=device, device_id_type=MESH)

    greet(partner)

    @pl.loop(0, 8)
    def _(i):
        greet(((i // 2) * 4 + (1 - zh) * 2 + i % 2, x * 4 + nearest))

    @pl.loop(1, 16)
    def _(i):
        t = (m + i) % 16
        greet(source(t))

    @pl.loop(1, 8)
    def _(i):
        greet(same_z(i))

    @pl.loop(1, 4)
    def _(i):
        greet((h, x * 4 + (zl + i) % 4))

    local = [
        pltpu.make_async_copy(ids_hbm, ids.at[h], loc_sem.at[0]),
        pltpu.make_async_copy(offs_hbm, offs.at[zh], loc_sem.at[17]),
        pltpu.make_async_copy(wsk_hbm, wself.at[place, 0], loc_sem.at[1]),
        pltpu.make_async_copy(wsv_hbm, wself.at[place, 1], loc_sem.at[2]),
        pltpu.make_async_copy(wsq_hbm, wself.at[place, 2], loc_sem.at[3]),
        pltpu.make_async_copy(wso_hbm, wso.at[h], loc_sem.at[4]),
        pltpu.make_async_copy(tab_hbm, tab, loc_sem.at[5]),
        pltpu.make_async_copy(wk_hbm, wk, loc_sem.at[6]),
        pltpu.make_async_copy(wv_hbm, wv, loc_sem.at[7]),
        pltpu.make_async_copy(wq_hbm, wq, loc_sem.at[8]),
        pltpu.make_async_copy(gain_hbm, gains, loc_sem.at[18]),
    ]
    for b in range(8):
        column = ((b // 2) * 4 + half_of(b % 4) * 2 + (b % 2)) * WIDE
        local.append(
            pltpu.make_async_copy(
                wo_hbm.at[:, pl.ds(pl.multiple_of(column, WIDE), WIDE)], wo.at[b], loc_sem.at[9 + b]
            )
        )
    for copy in local:
        copy.start()

    pl.semaphore_wait(barrier, 26 + jnp.where(at_edge, 16, 0))

    @pl.when(at_edge)
    def _():
        @pl.loop(0, 16)
        def _(i):
            device = (((i // 2) % 4) * 4 + (1 - zh) * 2 + i % 2, x * 4 + served + i // 8)
            remote(ids_hbm, ids.at[h], ids_s.at[8 + i], ids_r.at[h], device).start()

        for i in range(2):
            device = (y * 4 + (1 - zh) * 2 + c, x * 4 + served + i)
            remote(offs_hbm, offs.at[zh], offs_s.at[i], offs_r.at[0], device).start()

    @pl.loop(1, 8)
    def _(i):
        remote(ids_hbm, ids.at[h], ids_s.at[i], ids_r.at[h], same_z(i)).start()

    for copy in local[2:6]:
        copy.wait()
    for d in (1, 3, 2):
        remote(
            wself.at[place], wself.at[place], wself_s.at[d], wself_r.at[place], y_peer(d)
        ).start()
    remote(wself.at[place], wself.at[place], wself_s.at[0], wself_r.at[place], sibling).start()

    local[6].wait()
    local[7].wait()
    ktab[...] = dot(tab[...], wk[...]).astype(BF16)
    local[8].wait()
    vtab[...] = dot(tab[...], wv[...]).astype(BF16)
    local[9].wait()
    qtab[...] = dot(tab[...], wq[...]).astype(BF16)

    local[0].wait()
    local[1].wait()

    @pl.loop(1, 8)
    def _(i):
        other = (place + i) % 8
        b = (other // 2) * 4 + zh * 2 + other % 2
        arrived(ids.at[b], ids_r.at[b])

    vocab_iota = lax.broadcasted_iota(jnp.int32, (256, 128), 0)
    row_iota = lax.broadcasted_iota(jnp.int32, (128, 128), 0)

    def earlier(half, seen):
        def add(i, seen):
            b = (i // 2) * 4 + half * 2 + i % 2
            return sum(
                (jnp.where(vocab_iota == ids[b, r : r + 1, :], 1.0, 0.0) for r in range(4)), seen
            )

        return lax.fori_loop(0, y * 2, add, seen)

    def token_hot(b):
        return jnp.concatenate(
            [jnp.where(vocab_iota == ids[b, r : r + 1, :], 1.0, 0.0).astype(BF16) for r in range(4)],
            axis=1,
        )

    def masks(b, offsets):
        blocks = []
        for r in range(4):
            places = row_iota + (b * TOKENS + r * 128)
            blocks.append(
                jnp.concatenate(
                    [
                        jnp.where(places <= offsets, 1.0, 0.0).astype(BF16),
                        jnp.where(places == offsets, 1.0, 0.0).astype(BF16),
                    ],
                    axis=1,
                )
            )
        return jnp.concatenate(blocks, axis=0)

    seen = earlier(zh, jnp.zeros((256, 128), F32))
    near_hots = [token_hot(y * 4 + zh * 2 + q) for q in range(2)]

    @pl.loop(0, 8)
    def _(i):
        b = (i // 2) * 4 + (1 - zh) * 2 + i % 2
        arrived(ids.at[b], ids_r.at[b])

    arrived(offs.at[1 - zh], offs_r.at[0])

    cross_output_weights(0)

    offsets = jnp.concatenate([offs[0], offs[1]], axis=1)
    counted = jnp.zeros((256, 256), F32)
    for q in range(2):
        counted += dot(near_hots[q], masks(y * 4 + zh * 2 + q, offsets))
        b = y * 4 + (1 - zh) * 2 + q
        counted += dot(token_hot(b), masks(b, offsets))
    seen = earlier(1 - zh, seen)

    counts = (counted[:, :128] + jnp.sum(seen, axis=1, keepdims=True)).T
    hot = counted[:, 128:].T.astype(BF16)
    lat_hot[...] = hot
    latent_queries = dot(hot, qtab[...]).astype(BF16)
    present = counts > 0.0
    heads = []
    for hd in range(2):
        cols = slice(hd * HEAD_DIM, (hd + 1) * HEAD_DIM)
        scores = dot_nt(latent_queries[:, cols], ktab[:, cols]) * SCALE
        scores = jnp.where(present, scores, -1e30)
        top = jnp.max(scores, axis=1, keepdims=True)
        weights = jnp.where(present, jnp.exp(scores - top), 0.0) * counts
        total = jnp.sum(weights, axis=1, keepdims=True)
        heads.append(dot(weights.astype(BF16), vtab[:, cols]) / total)
    ctx[...] = jnp.concatenate(heads, axis=1).astype(BF16)

    for copy in local[11:]:
        copy.wait()
    turn = 3 - 2 * (zl % 2)
    z_order = [(zl + e) % 4 for e in (2, turn, 4 - turn, 0)]
    for other in z_order:
        for e in range(2):
            b = ((x + e) % 2) * 4 + other
            part = dot(ctx[...], wo[b]).astype(BF16)
            send1[b] = part[:ROWS]
            send1[8 + b] = part[ROWS:]
            for d in (1, 3) if e else (2, 0):
                t = ((x + d) % 4) * 4 + other

                def send(t=t):
                    remote(send1.at[t], recv1.at[m], rs1_s.at[t], rs1_r.at[m], peer(t)).start()

                if d or other is not z_order[3]:
                    send()
    recv1[m] = send1[m]

    own_block = ((m % 8) // 2) * 4 + zh * 2 + m % 2
    total = dot(
        lat_hot[pl.ds(pl.multiple_of((m // 8) * ROWS, ROWS), ROWS)],
        tab[:, pl.ds(pl.multiple_of(own_block * WIDE, WIDE), WIDE)],
    )

    @pl.loop(1, 16)
    def _(i):
        s = (m + i) % 16
        arrived(recv1.at[s], rs1_r.at[s])

    sums = recv1[0].astype(F32)
    for s in range(1, 16):
        sums += recv1[s].astype(F32)
    mid[m] = (total + sums).astype(BF16)

    order = (zl + 1 - 2 * (zl % 2), jnp.where(zl < 2, 2, 1), jnp.where(zl < 2, 3, 0))
    for e, other in enumerate(order):
        remote(
            mid.at[m], mid.at[m], ag_s.at[1 + e], ag_r.at[m], (h, x * 4 + other)
        ).start()
    for d in (1, 3, 2):
        remote(
            mid.at[m], mid.at[m], ag_s.at[4 + d], ag_r.at[m], (h, ((x + d) % 4) * 4 + zl)
        ).start()
    for d in (1, 3, 2):
        remote(wso.at[h], wso.at[h], wso_s.at[2 + d], wso_r.at[h], y_peer(d)).start()
    spread_far(0)

    for e, other in enumerate(order):
        t = x * 4 + other
        arrived(mid.at[t], ag_r.at[t])
        for d in (1, 3, 2):
            remote(
                mid.at[t], mid.at[t], ag_s.at[8 + e * 4 + d], ag_r.at[t], (h, ((x + d) % 4) * 4 + zl)
            ).start()

    cross_output_weights(1)

    for d in (1, 3, 2):
        slot = ((y + d) % 4) * 2 + c
        arrived(wself.at[slot], wself_r.at[slot])
        remote(
            wself.at[slot], wself.at[slot], wself_s.at[4 + d], wself_r.at[slot], sibling
        ).start()

    local[10].wait()
    gain_rows[...] = gains[...].astype(F32)

    for d in range(4):
        slot = d * 2 + 1 - c
        arrived(wself.at[slot], wself_r.at[slot])

    squares = jnp.zeros((128, 128), F32)
    key_part = jnp.zeros((128, WIDE), F32)
    for other in (zl, *order):
        for e in range(2):
            b = e * 4 + other
            for r in range(2):

                @pl.when(x != e + 2 * r)
                def _(t=r * 8 + b):
                    arrived(mid.at[t], ag_r.at[t])

            rows = jnp.concatenate([mid[b], mid[8 + b]], axis=0).astype(F32)
            squares += rows[:, :128] * rows[:, :128] + rows[:, 128:] * rows[:, 128:]
            first = ((b // 2) * 4 + zh * 2 + b % 2) * 2
            gain = [gain_rows[pl.ds(first + i, 1), :] for i in range(2)]
            scaled = (rows * jnp.concatenate(gain, axis=1)).astype(BF16)
            left[b] = scaled
            key_part += dot(scaled, wself[b, 0])

    def keep(j, part):
        zsend[j, 0] = part[:ROWS].astype(BF16)
        zsend[j, 1] = part[ROWS:].astype(BF16)
        return part

    def project(j):
        part = dot(left[0], wself[0, j])
        for b in range(1, 8):
            part += dot(left[b], wself[b, j])
        return keep(j, part)

    def push(j):
        for r in range(2):
            k = j * 2 + r
            remote(zsend.at[j, r], zrecv.at[j, r], zx_s.at[k], zx_r.at[k], partner).start()

    def pushed(j):
        for r in range(2):
            left_here(zsend.at[j, r], zx_s.at[j * 2 + r])

    parts = [keep(0, key_part)]
    push(0)
    square = jnp.broadcast_to(jnp.sum(squares, axis=1, keepdims=True), (128, 128)).T
    ss_send[...] = square[0:8]
    remote(ss_send, ss_recv, zx_s.at[6], zx_r.at[6], partner).start()
    parts.append(project(1))
    push(1)
    parts.append(project(2))

    own_bit = (m // 2) % 2
    home = (m // 4) * 2 + m % 2

    @pl.when(own_bit == zh)
    def _():
        away = (1 - zh) * 8 + home
        remote(mid.at[away], resid, res_s.at[0], res_r.at[0], partner).start()
        resid[...] = mid[zh * 8 + home]

    spread_far(1)

    arrived(ss_recv, zx_r.at[6])
    square = ss_send[0:1] + ss_recv[0:1]
    norm = lax.rsqrt(square * (1.0 / 4096.0) + 1e-05)
    norm = jnp.broadcast_to(norm, (128, 128)).T
    norm = jnp.concatenate([norm, norm], axis=1)

    for d in (1, 3, 2):
        slot = ((y + d) % 4) * 4 + zh * 2 + c
        arrived(wso.at[slot], wso_r.at[slot])
    for d in range(4):
        slot = d * 4 + zh * 2 + c
        remote(wso.at[slot], wso.at[slot], wso_s.at[16 + d], wso_r.at[slot], sibling).start()

    def kv_block(j, slot, r):
        return kv.at[j, pl.ds(pl.multiple_of(slot * 128 + r * ROWS, ROWS), ROWS), :]

    def whole(j, r):
        arrived(zrecv.at[j, r], zx_r.at[j * 2 + r])
        rows = slice(r * ROWS, (r + 1) * ROWS)
        return ((parts[j][rows] + zrecv[j, r].astype(F32)) * norm[rows]).astype(BF16)

    for j in range(2):
        for r in range(2):
            block = kv_block(j, place, r)
            block[...] = whole(j, r)
            k = (j * 2 + r) * 8
            for d in (1, 3, 2):
                remote(block, block, kv_s.at[k + d], kv_r.at[k + place], y_peer(d)).start()
            remote(block, block, kv_s.at[k], kv_r.at[k + place], sibling).start()
        if j == 0:
            push(2)

    def pass_block(j, r):
        k = (j * 2 + r) * 8
        for d in (1, 3, 2):
            slot = ((y + d) % 4) * 2 + c
            block = kv_block(j, slot, r)
            arrived(block, kv_r.at[k + slot])
            remote(block, block, kv_s.at[k + 4 + d], kv_r.at[k + slot], sibling).start()

    def wait_block(j, r):
        for d in range(4):
            slot = d * 2 + 1 - c
            arrived(kv_block(j, slot, r), kv_r.at[(j * 2 + r) * 8 + slot])

    pass_block(0, 0)
    pass_block(0, 1)
    queries[0:ROWS] = whole(2, 0)
    queries[ROWS:] = whole(2, 1)

    for d in (1, 3, 2):
        slot = ((y + d) % 4) * 4 + (1 - zh) * 2 + c
        for k in range(2):
            arrived(half_slot(slot, k), wso_r.at[16 + slot * 2 + k])
    for d in range(4):
        slot = d * 4 + (1 - zh) * 2 + c
        remote(wso.at[slot], wso.at[slot], wso_s.at[20 + d], wso_r.at[slot], sibling).start()

    wait_block(0, 0)
    wait_block(0, 1)

    key_lane = lax.broadcasted_iota(jnp.int32, (128, 1024), 1)
    key_in = key_lane % 128
    key_place = (
        (key_lane // 256) * 256 + ((key_lane // 128) % 2) * 64 + (key_in // 64) * 128 + key_in % 64
    )
    query_row = lax.broadcasted_iota(jnp.int32, (128, 1024), 0)
    query_place = y * 256 + c * 64 + (query_row // 64) * 128 + query_row % 64
    allowed = key_place <= query_place
    spread, totals = [], []
    for hd in range(2):
        cols = slice(hd * HEAD_DIM, (hd + 1) * HEAD_DIM)
        scores = dot_nt(queries[:, cols], kv[0, :, cols]) * SCALE
        scores = jnp.where(allowed, scores, -1e30)
        top = jnp.max(scores, axis=1, keepdims=True)
        weights = jnp.where(allowed, jnp.exp(scores - top), 0.0)
        totals.append(jnp.sum(weights, axis=1, keepdims=True))
        spread.append(weights.astype(BF16))

    pass_block(1, 0)
    pass_block(1, 1)

    wait_block(1, 0)
    wait_block(1, 1)

    heads = []
    for hd in range(2):
        cols = slice(hd * HEAD_DIM, (hd + 1) * HEAD_DIM)
        heads.append(dot(spread[hd], kv[1, :, cols]) / totals[hd])
    ctx[...] = jnp.concatenate(heads, axis=1).astype(BF16)

    for d in range(4):
        for half in range(2):
            slot = d * 4 + half * 2 + 1 - c
            arrived(wso.at[slot], wso_r.at[slot])

    def self_part(t):
        rows = pl.ds(pl.multiple_of(half_of(t % 4) * ROWS, ROWS), ROWS)
        return dot(ctx[rows, :], wso[t]).astype(BF16)

    for other in z_order:
        for d in (2, 1, 3, 0):
            t = ((x + d) % 4) * 4 + other
            if d or other is not z_order[3]:
                send2[t] = self_part(t)
                remote(send2.at[t], recv2.at[m], rs2_s.at[t], rs2_r.at[m], peer(t)).start()
    recv2[m] = self_part(m)

    @pl.when(own_bit != zh)
    def _():
        arrived(resid, res_r.at[0])

    @pl.loop(1, 16)
    def _(i):
        s = (m + i) % 16
        arrived(recv2.at[s], rs2_r.at[s])

    sums = resid[...].astype(F32)
    for s in range(16):
        sums += recv2[s].astype(F32)
    out_ref[...] = sums.astype(BF16)

    @pl.loop(1, 16)
    def _(i):
        s = (m + i) % 16
        left_here(send1.at[s], rs1_s.at[s])
        left_here(send2.at[s], rs2_s.at[s])

    @pl.when(at_edge)
    def _():
        @pl.loop(0, 16)
        def _(i):
            left_here(ids.at[h], ids_s.at[8 + i])

        for i in range(2):
            left_here(offs.at[0], offs_s.at[i])

    @pl.loop(1, 8)
    def _(i):
        left_here(ids.at[h], ids_s.at[i])

    @pl.loop(0, 8)
    def _(i):
        @pl.when(i != 4)
        def _():
            left_here(wself.at[0], wself_s.at[i])
            for k in range(4):
                left_here(kv_block(0, 0, 0), kv_s.at[k * 8 + i])

    for i in (0, 1, 7, 8, 9, 11, 12, 13):
        left_here(half_slot(0, 0), wso_s.at[i])
    for i in (3, 4, 5, 16, 17, 18, 19, 20, 21, 22, 23):
        left_here(wso.at[0], wso_s.at[i])

    for i in (1, 2, 3, 5, 6, 7, 9, 10, 11, 13, 14, 15, 17, 18, 19):
        left_here(mid.at[0], ag_s.at[i])
    pushed(0)
    pushed(1)
    pushed(2)
    left_here(ss_send, zx_s.at[6])

    @pl.when(own_bit == zh)
    def _():
        left_here(resid, res_s.at[0])


def per_device(
    history_ids, latent_offsets, byte_table, w_query, w_key, w_value, w_out, norm_gain,
    w_self_query, w_self_key, w_self_value, w_self_out,
):
    vmem = pl.BlockSpec(memory_space=pltpu.VMEM)
    hbm = pl.BlockSpec(memory_space=pl.ANY)
    dma = pltpu.SemaphoreType.DMA
    scratch = [
        pltpu.VMEM((16, 4, 128), jnp.int32),
        pltpu.VMEM((2, 1, 64), jnp.int32),
        pltpu.VMEM((32, 128), BF16),
        pltpu.VMEM((32, 128), F32),
        pltpu.VMEM((256, 4096), BF16),
        pltpu.VMEM((4096, 256), BF16),
        pltpu.VMEM((4096, 256), BF16),
        pltpu.VMEM((4096, 256), BF16),
        pltpu.VMEM((8, 256, 256), BF16),
        pltpu.VMEM((8, 3, 256, 256), BF16),
        pltpu.VMEM((16, 256, 256), BF16),
        pltpu.VMEM((256, 256), BF16),
        pltpu.VMEM((256, 256), BF16),
        pltpu.VMEM((256, 256), BF16),
        pltpu.VMEM((128, 256), BF16),
        pltpu.VMEM((16, ROWS, WIDE), BF16),
        pltpu.VMEM((16, ROWS, WIDE), BF16),
        pltpu.VMEM((16, ROWS, WIDE), BF16),
        pltpu.VMEM((8, 128, WIDE), BF16),
        pltpu.VMEM((3, 2, ROWS, WIDE), BF16),
        pltpu.VMEM((3, 2, ROWS, WIDE), BF16),
        pltpu.VMEM((8, 128), F32),
        pltpu.VMEM((8, 128), F32),
        pltpu.VMEM((2, 1024, WIDE), BF16),
        pltpu.VMEM((128, WIDE), BF16),
        pltpu.VMEM((128, WIDE), BF16),
        pltpu.VMEM((16, ROWS, WIDE), BF16),
        pltpu.VMEM((16, ROWS, WIDE), BF16),
        pltpu.VMEM((ROWS, WIDE), BF16),
    ] + [dma((n,)) for n in (
        19, 24, 16, 8, 8, 24, 48, 16, 16, 20, 16, 7, 7, 32, 32, 16, 16, 1, 1, 2, 1
    )]
    return pl.pallas_call(
        kernel,
        out_shape=jax.ShapeDtypeStruct((ROWS, WIDE), BF16),
        in_specs=[hbm] * 12,
        out_specs=vmem,
        scratch_shapes=scratch,
        compiler_params=pltpu.CompilerParams(
            collective_id=0, has_side_effects=True, vmem_limit_bytes=56 * 1024 * 1024
        ),
        cost_estimate=pl.CostEstimate(
            flops=5_000_000_000, bytes_accessed=12_000_000, transcendentals=400_000
        ),
    )(
        history_ids.reshape(4, 128), latent_offsets.reshape(1, 64), norm_gain.reshape(32, 128),
        byte_table, w_query, w_key, w_value, w_out,
        w_self_query, w_self_key, w_self_value, w_self_out,
    )


def solution(mesh):
    return jax.shard_map(
        per_device,
        mesh=mesh,
        in_specs=(
            P("hist"),
            P("hist"),
            P(),
            P(None, "mp"),
            P(None, "mp"),
            P(None, "mp"),
            P("mp", None),
            P(),
            P("hist", "mp"),
            P("hist", "mp"),
            P("hist", "mp"),
            P("mp", "hist"),
        ),
        out_specs=P("hist", "mp"),
        check_vma=False,
    )
```

```python
import functools
import math

import jax
import jax.numpy as jnp
from jax import lax
from jax.experimental import pallas as pl
from jax.experimental.pallas import tpu as pltpu
from jax.sharding import PartitionSpec as P

HEAD_DIM = 128
MESH = pl.DeviceIdType.MESH
BF16 = jnp.bfloat16
F32 = jnp.float32
SCALE = 1.0 / math.sqrt(HEAD_DIM)
ROWS = 64
WIDE = 256
TOKENS = 512
NT = (((1,), (1,)), ((), ()))


def dot(a, b):
    return jnp.dot(a, b, preferred_element_type=F32)


def dot_nt(a, b):
    return lax.dot_general(a, b, NT, preferred_element_type=F32)


def kernel(
    ids_hbm, offs_hbm, gain_hbm, tab_hbm, wq_hbm, wk_hbm, wv_hbm, wo_hbm,
    wsq_hbm, wsk_hbm, wsv_hbm, wso_hbm,
    out_ref,
    ids, offs, gains, gain_rows, tab, wq, wk, wv, wo, wself, wso, ktab, qtab, vtab, lat_hot,
    send1, recv1, mid, left, zsend, zrecv, ss_send, ss_recv, kv, queries, ctx, send2, recv2, resid,
    loc_sem, ids_s, ids_r, wself_s, wself_r, wso_s, wso_r, rs1_s, rs1_r, ag_s, ag_r,
    zx_s, zx_r, kv_s, kv_r, rs2_s, rs2_r, res_s, res_r, offs_s, offs_r,
):
    h = lax.axis_index("hist")
    m = lax.axis_index("mp")
    y, zh, c = h // 4, (h // 2) % 2, h % 2
    x, zl = m // 4, m % 4
    place = y * 2 + c
    at_edge = (zl == 0) | (zl == 3)
    nearest = jnp.where(zl < 2, 3, 0)
    served = jnp.where(zl == 0, 2, 0)

    def half_of(target_zl):
        own_pair = (target_zl // 2) == (zl // 2)
        inner = (zl == 1) | (zl == 2)
        return jnp.where(own_pair | inner, zh, 1 - zh)

    def peer(t):
        return (y * 4 + half_of(t % 4) * 2 + c, t)

    def source(t):
        return (y * 4 + jnp.where(t % 4 == nearest, 1 - zh, zh) * 2 + c, t)

    partner = (y * 4 + (1 - zh) * 2 + c, m)
    sibling = (y * 4 + zh * 2 + 1 - c, m)

    def same_z(i):
        other = (place + i) % 8
        return ((other // 2) * 4 + zh * 2 + other % 2, m)

    def y_peer(d):
        return (((y + d) % 4) * 4 + zh * 2 + c, m)

    def remote(src, dst, s, r, device):
        return pltpu.make_async_remote_copy(
            src_ref=src, dst_ref=dst, send_sem=s, recv_sem=r, device_id=device, device_id_type=MESH
        )

    def arrived(ref, sem):
        remote(ref, ref, sem, sem, partner).wait_recv()

    def left_here(ref, sem):
        remote(ref, ref, sem, sem, partner).wait_send()

    far = y * 4 + (1 - zh) * 2 + c

    def half_slot(slot, k):
        return wso.at[slot, pl.ds(k * 128, 128)]

    def cross_output_weights(k):
        part = half_slot(h, k)
        remote(part, part, wso_s.at[k], wso_r.at[16 + h * 2 + k], partner).start()

    def spread_far(k):
        part = half_slot(far, k)
        arrived(part, wso_r.at[16 + far * 2 + k])
        for d in (1, 3, 2):
            remote(
                part, part, wso_s.at[6 + k * 4 + d], wso_r.at[16 + far * 2 + k], y_peer(d)
            ).start()

    barrier = pltpu.get_barrier_semaphore()

    def greet(device):
        pl.semaphore_signal(barrier, inc=1, device_id=device, device_id_type=MESH)

    greet(partner)

    @pl.loop(0, 8)
    def _(i):
        greet(((i // 2) * 4 + (1 - zh) * 2 + i % 2, x * 4 + nearest))

    @pl.loop(1, 16)
    def _(i):
        t = (m + i) % 16
        greet(source(t))

    @pl.loop(1, 8)
    def _(i):
        greet(same_z(i))

    @pl.loop(1, 4)
    def _(i):
        greet((h, x * 4 + (zl + i) % 4))

    local = [
        pltpu.make_async_copy(ids_hbm, ids.at[h], loc_sem.at[0]),
        pltpu.make_async_copy(offs_hbm, offs.at[zh], loc_sem.at[17]),
        pltpu.make_async_copy(wsk_hbm, wself.at[place, 0], loc_sem.at[1]),
        pltpu.make_async_copy(wsv_hbm, wself.at[place, 1], loc_sem.at[2]),
        pltpu.make_async_copy(wsq_hbm, wself.at[place, 2], loc_sem.at[3]),
        pltpu.make_async_copy(wso_hbm, wso.at[h], loc_sem.at[4]),
        pltpu.make_async_copy(tab_hbm, tab, loc_sem.at[5]),
        pltpu.make_async_copy(wk_hbm, wk, loc_sem.at[6]),
        pltpu.make_async_copy(wv_hbm, wv, loc_sem.at[7]),
        pltpu.make_async_copy(wq_hbm, wq, loc_sem.at[8]),
        pltpu.make_async_copy(gain_hbm, gains, loc_sem.at[18]),
    ]
    for b in range(8):
        column = ((b // 2) * 4 + half_of(b % 4) * 2 + (b % 2)) * WIDE
        local.append(
            pltpu.make_async_copy(
                wo_hbm.at[:, pl.ds(pl.multiple_of(column, WIDE), WIDE)], wo.at[b], loc_sem.at[9 + b]
            )
        )
    for copy in local:
        copy.start()

    pl.semaphore_wait(barrier, 26 + jnp.where(at_edge, 16, 0))

    @pl.when(at_edge)
    def _():
        @pl.loop(0, 16)
        def _(i):
            device = (((i // 2) % 4) * 4 + (1 - zh) * 2 + i % 2, x * 4 + served + i // 8)
            remote(ids_hbm, ids.at[h], ids_s.at[8 + i], ids_r.at[h], device).start()

        for i in range(2):
            device = (y * 4 + (1 - zh) * 2 + c, x * 4 + served + i)
            remote(offs_hbm, offs.at[zh], offs_s.at[i], offs_r.at[0], device).start()

    @pl.loop(1, 8)
    def _(i):
        remote(ids_hbm, ids.at[h], ids_s.at[i], ids_r.at[h], same_z(i)).start()

    for copy in local[2:6]:
        copy.wait()
    for d in (1, 3, 2):
        remote(
            wself.at[place], wself.at[place], wself_s.at[d], wself_r.at[place], y_peer(d)
        ).start()
    remote(wself.at[place], wself.at[place], wself_s.at[0], wself_r.at[place], sibling).start()

    local[6].wait()
    local[7].wait()
    ktab[...] = dot(tab[...], wk[...]).astype(BF16)
    local[8].wait()
    vtab[...] = dot(tab[...], wv[...]).astype(BF16)
    local[9].wait()
    qtab[...] = dot(tab[...], wq[...]).astype(BF16)

    local[0].wait()
    local[1].wait()

    @pl.loop(1, 8)
    def _(i):
        other = (place + i) % 8
        b = (other // 2) * 4 + zh * 2 + other % 2
        arrived(ids.at[b], ids_r.at[b])

    vocab_iota = lax.broadcasted_iota(jnp.int32, (256, 128), 0)
    row_iota = lax.broadcasted_iota(jnp.int32, (128, 128), 0)

    def earlier(half, seen):
        def add(i, seen):
            b = (i // 2) * 4 + half * 2 + i % 2
            return sum(
                (jnp.where(vocab_iota == ids[b, r : r + 1, :], 1.0, 0.0) for r in range(4)), seen
            )

        return lax.fori_loop(0, y * 2, add, seen)

    def token_hot(b):
        return jnp.concatenate(
            [jnp.where(vocab_iota == ids[b, r : r + 1, :], 1.0, 0.0).astype(BF16) for r in range(4)],
            axis=1,
        )

    def masks(b, offsets):
        blocks = []
        for r in range(4):
            places = row_iota + (b * TOKENS + r * 128)
            blocks.append(
                jnp.concatenate(
                    [
                        jnp.where(places <= offsets, 1.0, 0.0).astype(BF16),
                        jnp.where(places == offsets, 1.0, 0.0).astype(BF16),
                    ],
                    axis=1,
                )
            )
        return jnp.concatenate(blocks, axis=0)

    seen = earlier(zh, jnp.zeros((256, 128), F32))
    near_hots = [token_hot(y * 4 + zh * 2 + q) for q in range(2)]

    @pl.loop(0, 8)
    def _(i):
        b = (i // 2) * 4 + (1 - zh) * 2 + i % 2
        arrived(ids.at[b], ids_r.at[b])

    arrived(offs.at[1 - zh], offs_r.at[0])

    cross_output_weights(0)

    offsets = jnp.concatenate([offs[0], offs[1]], axis=1)
    counted = jnp.zeros((256, 256), F32)
    for q in range(2):
        counted += dot(near_hots[q], masks(y * 4 + zh * 2 + q, offsets))
        b = y * 4 + (1 - zh) * 2 + q
        counted += dot(token_hot(b), masks(b, offsets))
    seen = earlier(1 - zh, seen)

    counts = (counted[:, :128] + jnp.sum(seen, axis=1, keepdims=True)).T
    hot = counted[:, 128:].T.astype(BF16)
    lat_hot[...] = hot
    latent_queries = dot(hot, qtab[...]).astype(BF16)
    present = counts > 0.0
    heads = []
    for hd in range(2):
        cols = slice(hd * HEAD_DIM, (hd + 1) * HEAD_DIM)
        scores = dot_nt(latent_queries[:, cols], ktab[:, cols]) * SCALE
        scores = jnp.where(present, scores, -1e30)
        top = jnp.max(scores, axis=1, keepdims=True)
        weights = jnp.where(present, jnp.exp(scores - top), 0.0) * counts
        total = jnp.sum(weights, axis=1, keepdims=True)
        heads.append(dot(weights.astype(BF16), vtab[:, cols]) / total)
    ctx[...] = jnp.concatenate(heads, axis=1).astype(BF16)

    for copy in local[11:]:
        copy.wait()
    turn = 3 - 2 * (zl % 2)
    z_order = [(zl + e) % 4 for e in (2, turn, 4 - turn, 0)]
    for other in z_order:
        for e in (1, 0):
            b = ((x + e) % 2) * 4 + other
            part = dot(ctx[...], wo[b]).astype(BF16)
            send1[b] = part[:ROWS]
            send1[8 + b] = part[ROWS:]
            for d in (1, 3) if e else (2, 0):
                t = ((x + d) % 4) * 4 + other

                def send(t=t):
                    remote(send1.at[t], recv1.at[m], rs1_s.at[t], rs1_r.at[m], peer(t)).start()

                if d or other is not z_order[3]:
                    send()
    recv1[m] = send1[m]

    own_block = ((m % 8) // 2) * 4 + zh * 2 + m % 2
    total = dot(
        lat_hot[pl.ds(pl.multiple_of((m // 8) * ROWS, ROWS), ROWS)],
        tab[:, pl.ds(pl.multiple_of(own_block * WIDE, WIDE), WIDE)],
    )

    @pl.loop(1, 16)
    def _(i):
        s = (m + i) % 16
        arrived(recv1.at[s], rs1_r.at[s])

    sums = recv1[0].astype(F32)
    for s in range(1, 16):
        sums += recv1[s].astype(F32)
    mid[m] = (total + sums).astype(BF16)

    order = (zl + 1 - 2 * (zl % 2), jnp.where(zl < 2, 2, 1), jnp.where(zl < 2, 3, 0))
    for d in (1, 3, 2):
        remote(
            mid.at[m], mid.at[m], ag_s.at[4 + d], ag_r.at[m], (h, ((x + d) % 4) * 4 + zl)
        ).start()
    for e, other in enumerate(order):
        remote(
            mid.at[m], mid.at[m], ag_s.at[1 + e], ag_r.at[m], (h, x * 4 + other)
        ).start()

    for d in (1, 3, 2):
        remote(wso.at[h], wso.at[h], wso_s.at[2 + d], wso_r.at[h], y_peer(d)).start()
    spread_far(0)

    for e, other in enumerate(order):
        t = x * 4 + other
        arrived(mid.at[t], ag_r.at[t])
        for d in (1, 3, 2):
            remote(
                mid.at[t], mid.at[t], ag_s.at[8 + e * 4 + d], ag_r.at[t], (h, ((x + d) % 4) * 4 + zl)
            ).start()

    cross_output_weights(1)

    for d in (1, 3, 2):
        slot = ((y + d) % 4) * 2 + c
        arrived(wself.at[slot], wself_r.at[slot])
        remote(
            wself.at[slot], wself.at[slot], wself_s.at[4 + d], wself_r.at[slot], sibling
        ).start()

    local[10].wait()
    gain_rows[...] = gains[...].astype(F32)

    for d in range(4):
        slot = d * 2 + 1 - c
        arrived(wself.at[slot], wself_r.at[slot])

    squares = jnp.zeros((128, 128), F32)
    key_part = jnp.zeros((128, WIDE), F32)
    for other in (zl, *order):
        for e in range(2):
            b = e * 4 + other
            for r in range(2):

                @pl.when(x != e + 2 * r)
                def _(t=r * 8 + b):
                    arrived(mid.at[t], ag_r.at[t])

            rows = jnp.concatenate([mid[b], mid[8 + b]], axis=0).astype(F32)
            squares += rows[:, :128] * rows[:, :128] + rows[:, 128:] * rows[:, 128:]
            first = ((b // 2) * 4 + zh * 2 + b % 2) * 2
            gain = [gain_rows[pl.ds(first + i, 1), :] for i in range(2)]
            scaled = (rows * jnp.concatenate(gain, axis=1)).astype(BF16)
            left[b] = scaled
            key_part += dot(scaled, wself[b, 0])

    def keep(j, part):
        zsend[j, 0] = part[:ROWS].astype(BF16)
        zsend[j, 1] = part[ROWS:].astype(BF16)
        return part

    def project(j):
        part = dot(left[0], wself[0, j])
        for b in range(1, 8):
            part += dot(left[b], wself[b, j])
        return keep(j, part)

    def push(j):
        for r in range(2):
            k = j * 2 + r
            remote(zsend.at[j, r], zrecv.at[j, r], zx_s.at[k], zx_r.at[k], partner).start()

    def pushed(j):
        for r in range(2):
            left_here(zsend.at[j, r], zx_s.at[j * 2 + r])

    parts = [keep(0, key_part)]
    push(0)
    square = jnp.broadcast_to(jnp.sum(squares, axis=1, keepdims=True), (128, 128)).T
    ss_send[...] = square[0:8]
    remote(ss_send, ss_recv, zx_s.at[6], zx_r.at[6], partner).start()
    parts.append(project(1))
    push(1)
    parts.append(project(2))

    own_bit = (m // 2) % 2
    home = (m // 4) * 2 + m % 2

    @pl.when(own_bit == zh)
    def _():
        away = (1 - zh) * 8 + home
        remote(mid.at[away], resid, res_s.at[0], res_r.at[0], partner).start()
        resid[...] = mid[zh * 8 + home]

    spread_far(1)

    arrived(ss_recv, zx_r.at[6])
    square = ss_send[0:1] + ss_recv[0:1]
    norm = lax.rsqrt(square * (1.0 / 4096.0) + 1e-05)
    norm = jnp.broadcast_to(norm, (128, 128)).T
    norm = jnp.concatenate([norm, norm], axis=1)

    for d in (1, 3, 2):
        slot = ((y + d) % 4) * 4 + zh * 2 + c
        arrived(wso.at[slot], wso_r.at[slot])
    for d in range(4):
        slot = d * 4 + zh * 2 + c
        remote(wso.at[slot], wso.at[slot], wso_s.at[16 + d], wso_r.at[slot], sibling).start()

    def kv_block(j, slot, r):
        return kv.at[j, pl.ds(pl.multiple_of(slot * 128 + r * ROWS, ROWS), ROWS), :]

    def whole(j, r):
        arrived(zrecv.at[j, r], zx_r.at[j * 2 + r])
        rows = slice(r * ROWS, (r + 1) * ROWS)
        return ((parts[j][rows] + zrecv[j, r].astype(F32)) * norm[rows]).astype(BF16)

    for j in range(2):
        for r in range(2):
            block = kv_block(j, place, r)
            block[...] = whole(j, r)
            k = (j * 2 + r) * 8
            for d in (1, 3, 2):
                remote(block, block, kv_s.at[k + d], kv_r.at[k + place], y_peer(d)).start()
            remote(block, block, kv_s.at[k], kv_r.at[k + place], sibling).start()
        if j == 0:
            push(2)

    def pass_block(j, r):
        k = (j * 2 + r) * 8
        for d in (1, 3, 2):
            slot = ((y + d) % 4) * 2 + c
            block = kv_block(j, slot, r)
            arrived(block, kv_r.at[k + slot])
            remote(block, block, kv_s.at[k + 4 + d], kv_r.at[k + slot], sibling).start()

    def wait_block(j, r):
        for d in range(4):
            slot = d * 2 + 1 - c
            arrived(kv_block(j, slot, r), kv_r.at[(j * 2 + r) * 8 + slot])

    pass_block(0, 0)
    pass_block(0, 1)
    queries[0:ROWS] = whole(2, 0)
    queries[ROWS:] = whole(2, 1)

    for d in (1, 3, 2):
        slot = ((y + d) % 4) * 4 + (1 - zh) * 2 + c
        for k in range(2):
            arrived(half_slot(slot, k), wso_r.at[16 + slot * 2 + k])
    for d in range(4):
        slot = d * 4 + (1 - zh) * 2 + c
        remote(wso.at[slot], wso.at[slot], wso_s.at[20 + d], wso_r.at[slot], sibling).start()

    wait_block(0, 0)
    wait_block(0, 1)

    key_lane = lax.broadcasted_iota(jnp.int32, (128, 1024), 1)
    key_in = key_lane % 128
    key_place = (
        (key_lane // 256) * 256 + ((key_lane // 128) % 2) * 64 + (key_in // 64) * 128 + key_in % 64
    )
    query_row = lax.broadcasted_iota(jnp.int32, (128, 1024), 0)
    query_place = y * 256 + c * 64 + (query_row // 64) * 128 + query_row % 64
    allowed = key_place <= query_place
    spread, totals = [], []
    for hd in range(2):
        cols = slice(hd * HEAD_DIM, (hd + 1) * HEAD_DIM)
        scores = dot_nt(queries[:, cols], kv[0, :, cols]) * SCALE
        scores = jnp.where(allowed, scores, -1e30)
        top = jnp.max(scores, axis=1, keepdims=True)
        weights = jnp.where(allowed, jnp.exp(scores - top), 0.0)
        totals.append(jnp.sum(weights, axis=1, keepdims=True))
        spread.append(weights.astype(BF16))

    pass_block(1, 0)
    pass_block(1, 1)

    wait_block(1, 0)
    wait_block(1, 1)

    heads = []
    for hd in range(2):
        cols = slice(hd * HEAD_DIM, (hd + 1) * HEAD_DIM)
        heads.append(dot(spread[hd], kv[1, :, cols]) / totals[hd])
    ctx[...] = jnp.concatenate(heads, axis=1).astype(BF16)

    for d in range(4):
        for half in range(2):
            slot = d * 4 + half * 2 + 1 - c
            arrived(wso.at[slot], wso_r.at[slot])

    def self_part(t):
        rows = pl.ds(pl.multiple_of(half_of(t % 4) * ROWS, ROWS), ROWS)
        return dot(ctx[rows, :], wso[t]).astype(BF16)

    for other in z_order:
        for d in (2, 1, 3, 0):
            t = ((x + d) % 4) * 4 + other
            if d or other is not z_order[3]:
                send2[t] = self_part(t)
                remote(send2.at[t], recv2.at[m], rs2_s.at[t], rs2_r.at[m], peer(t)).start()
    recv2[m] = self_part(m)

    @pl.when(own_bit != zh)
    def _():
        arrived(resid, res_r.at[0])

    @pl.loop(1, 16)
    def _(i):
        s = (m + i) % 16
        arrived(recv2.at[s], rs2_r.at[s])

    sums = resid[...].astype(F32)
    for s in range(16):
        sums += recv2[s].astype(F32)
    out_ref[...] = sums.astype(BF16)

    @pl.loop(1, 16)
    def _(i):
        s = (m + i) % 16
        left_here(send1.at[s], rs1_s.at[s])
        left_here(send2.at[s], rs2_s.at[s])

    @pl.when(at_edge)
    def _():
        @pl.loop(0, 16)
        def _(i):
            left_here(ids.at[h], ids_s.at[8 + i])

        for i in range(2):
            left_here(offs.at[0], offs_s.at[i])

    @pl.loop(1, 8)
    def _(i):
        left_here(ids.at[h], ids_s.at[i])

    @pl.loop(0, 8)
    def _(i):
        @pl.when(i != 4)
        def _():
            left_here(wself.at[0], wself_s.at[i])
            for k in range(4):
                left_here(kv_block(0, 0, 0), kv_s.at[k * 8 + i])

    for i in (0, 1, 7, 8, 9, 11, 12, 13):
        left_here(half_slot(0, 0), wso_s.at[i])
    for i in (3, 4, 5, 16, 17, 18, 19, 20, 21, 22, 23):
        left_here(wso.at[0], wso_s.at[i])

    for i in (1, 2, 3, 5, 6, 7, 9, 10, 11, 13, 14, 15, 17, 18, 19):
        left_here(mid.at[0], ag_s.at[i])
    pushed(0)
    pushed(1)
    pushed(2)
    left_here(ss_send, zx_s.at[6])

    @pl.when(own_bit == zh)
    def _():
        left_here(resid, res_s.at[0])


def per_device(
    history_ids, latent_offsets, byte_table, w_query, w_key, w_value, w_out, norm_gain,
    w_self_query, w_self_key, w_self_value, w_self_out,
):
    vmem = pl.BlockSpec(memory_space=pltpu.VMEM)
    hbm = pl.BlockSpec(memory_space=pl.ANY)
    dma = pltpu.SemaphoreType.DMA
    scratch = [
        pltpu.VMEM((16, 4, 128), jnp.int32),
        pltpu.VMEM((2, 1, 64), jnp.int32),
        pltpu.VMEM((32, 128), BF16),
        pltpu.VMEM((32, 128), F32),
        pltpu.VMEM((256, 4096), BF16),
        pltpu.VMEM((4096, 256), BF16),
        pltpu.VMEM((4096, 256), BF16),
        pltpu.VMEM((4096, 256), BF16),
        pltpu.VMEM((8, 256, 256), BF16),
        pltpu.VMEM((8, 3, 256, 256), BF16),
        pltpu.VMEM((16, 256, 256), BF16),
        pltpu.VMEM((256, 256), BF16),
        pltpu.VMEM((256, 256), BF16),
        pltpu.VMEM((256, 256), BF16),
        pltpu.VMEM((128, 256), BF16),
        pltpu.VMEM((16, ROWS, WIDE), BF16),
        pltpu.VMEM((16, ROWS, WIDE), BF16),
        pltpu.VMEM((16, ROWS, WIDE), BF16),
        pltpu.VMEM((8, 128, WIDE), BF16),
        pltpu.VMEM((3, 2, ROWS, WIDE), BF16),
        pltpu.VMEM((3, 2, ROWS, WIDE), BF16),
        pltpu.VMEM((8, 128), F32),
        pltpu.VMEM((8, 128), F32),
        pltpu.VMEM((2, 1024, WIDE), BF16),
        pltpu.VMEM((128, WIDE), BF16),
        pltpu.VMEM((128, WIDE), BF16),
        pltpu.VMEM((16, ROWS, WIDE), BF16),
        pltpu.VMEM((16, ROWS, WIDE), BF16),
        pltpu.VMEM((ROWS, WIDE), BF16),
    ] + [dma((n,)) for n in (
        19, 24, 16, 8, 8, 24, 48, 16, 16, 20, 16, 7, 7, 32, 32, 16, 16, 1, 1, 2, 1
    )]
    return pl.pallas_call(
        kernel,
        out_shape=jax.ShapeDtypeStruct((ROWS, WIDE), BF16),
        in_specs=[hbm] * 12,
        out_specs=vmem,
        scratch_shapes=scratch,
        compiler_params=pltpu.CompilerParams(
            collective_id=0, has_side_effects=True, vmem_limit_bytes=56 * 1024 * 1024
        ),
        cost_estimate=pl.CostEstimate(
            flops=5_000_000_000, bytes_accessed=12_000_000, transcendentals=400_000
        ),
    )(
        history_ids.reshape(4, 128), latent_offsets.reshape(1, 64), norm_gain.reshape(32, 128),
        byte_table, w_query, w_key, w_value, w_out,
        w_self_query, w_self_key, w_self_value, w_self_out,
    )


def solution(mesh):
    return jax.shard_map(
        per_device,
        mesh=mesh,
        in_specs=(
            P("hist"),
            P("hist"),
            P(),
            P(None, "mp"),
            P(None, "mp"),
            P(None, "mp"),
            P("mp", None),
            P(),
            P("hist", "mp"),
            P("hist", "mp"),
            P("hist", "mp"),
            P("mp", "hist"),
        ),
        out_specs=P("hist", "mp"),
        check_vma=False,
    )
```

```python
import functools
import math

import jax
import jax.numpy as jnp
from jax import lax
from jax.experimental import pallas as pl
from jax.experimental.pallas import tpu as pltpu
from jax.sharding import PartitionSpec as P

HEAD_DIM = 128
MESH = pl.DeviceIdType.MESH
BF16 = jnp.bfloat16
F32 = jnp.float32
SCALE = 1.0 / math.sqrt(HEAD_DIM)
ROWS = 64
WIDE = 256
TOKENS = 512
NT = (((1,), (1,)), ((), ()))


def dot(a, b):
    return jnp.dot(a, b, preferred_element_type=F32)


def dot_nt(a, b):
    return lax.dot_general(a, b, NT, preferred_element_type=F32)


def kernel(
    ids_hbm, offs_hbm, gain_hbm, tab_hbm, wq_hbm, wk_hbm, wv_hbm, wo_hbm,
    wsq_hbm, wsk_hbm, wsv_hbm, wso_hbm,
    out_ref,
    ids, offs, gains, gain_rows, tab, wq, wk, wv, wo, wself, wso, ktab, qtab, vtab, lat_hot,
    send1, recv1, mid, left, zsend, zrecv, ss_send, ss_recv, kv, queries, ctx, send2, recv2, resid,
    loc_sem, ids_s, ids_r, wself_s, wself_r, wso_s, wso_r, rs1_s, rs1_r, ag_s, ag_r,
    zx_s, zx_r, kv_s, kv_r, rs2_s, rs2_r, res_s, res_r, offs_s, offs_r,
):
    h = lax.axis_index("hist")
    m = lax.axis_index("mp")
    y, zh, c = h // 4, (h // 2) % 2, h % 2
    x, zl = m // 4, m % 4
    place = y * 2 + c
    at_edge = (zl == 0) | (zl == 3)
    nearest = jnp.where(zl < 2, 3, 0)
    served = jnp.where(zl == 0, 2, 0)

    def half_of(target_zl):
        own_pair = (target_zl // 2) == (zl // 2)
        inner = (zl == 1) | (zl == 2)
        return jnp.where(own_pair | inner, zh, 1 - zh)

    def peer(t):
        return (y * 4 + half_of(t % 4) * 2 + c, t)

    def source(t):
        return (y * 4 + jnp.where(t % 4 == nearest, 1 - zh, zh) * 2 + c, t)

    partner = (y * 4 + (1 - zh) * 2 + c, m)
    sibling = (y * 4 + zh * 2 + 1 - c, m)

    def same_z(i):
        other = (place + i) % 8
        return ((other // 2) * 4 + zh * 2 + other % 2, m)

    def y_peer(d):
        return (((y + d) % 4) * 4 + zh * 2 + c, m)

    def remote(src, dst, s, r, device):
        return pltpu.make_async_remote_copy(
            src_ref=src, dst_ref=dst, send_sem=s, recv_sem=r, device_id=device, device_id_type=MESH
        )

    def arrived(ref, sem):
        remote(ref, ref, sem, sem, partner).wait_recv()

    def left_here(ref, sem):
        remote(ref, ref, sem, sem, partner).wait_send()

    far = y * 4 + (1 - zh) * 2 + c

    def half_slot(slot, k):
        return wso.at[slot, pl.ds(k * 128, 128)]

    def cross_output_weights(k):
        part = half_slot(h, k)
        remote(part, part, wso_s.at[k], wso_r.at[16 + h * 2 + k], partner).start()

    def spread_far(k):
        part = half_slot(far, k)
        arrived(part, wso_r.at[16 + far * 2 + k])
        for d in (1, 3, 2):
            remote(
                part, part, wso_s.at[6 + k * 4 + d], wso_r.at[16 + far * 2 + k], y_peer(d)
            ).start()

    barrier = pltpu.get_barrier_semaphore()

    def greet(device):
        pl.semaphore_signal(barrier, inc=1, device_id=device, device_id_type=MESH)

    greet(partner)

    @pl.loop(0, 8)
    def _(i):
        greet(((i // 2) * 4 + (1 - zh) * 2 + i % 2, x * 4 + nearest))

    @pl.loop(1, 16)
    def _(i):
        t = (m + i) % 16
        greet(source(t))

    @pl.loop(1, 8)
    def _(i):
        greet(same_z(i))

    @pl.loop(1, 4)
    def _(i):
        greet((h, x * 4 + (zl + i) % 4))

    local = [
        pltpu.make_async_copy(ids_hbm, ids.at[h], loc_sem.at[0]),
        pltpu.make_async_copy(offs_hbm, offs.at[zh], loc_sem.at[17]),
        pltpu.make_async_copy(wsk_hbm, wself.at[place, 0], loc_sem.at[1]),
        pltpu.make_async_copy(wsv_hbm, wself.at[place, 1], loc_sem.at[2]),
        pltpu.make_async_copy(wsq_hbm, wself.at[place, 2], loc_sem.at[3]),
        pltpu.make_async_copy(wso_hbm, wso.at[h], loc_sem.at[4]),
        pltpu.make_async_copy(tab_hbm, tab, loc_sem.at[5]),
        pltpu.make_async_copy(wk_hbm, wk, loc_sem.at[6]),
        pltpu.make_async_copy(wv_hbm, wv, loc_sem.at[7]),
        pltpu.make_async_copy(wq_hbm, wq, loc_sem.at[8]),
        pltpu.make_async_copy(gain_hbm, gains, loc_sem.at[18]),
    ]
    for b in range(8):
        column = ((b // 2) * 4 + half_of(b % 4) * 2 + (b % 2)) * WIDE
        local.append(
            pltpu.make_async_copy(
                wo_hbm.at[:, pl.ds(pl.multiple_of(column, WIDE), WIDE)], wo.at[b], loc_sem.at[9 + b]
            )
        )
    for copy in local:
        copy.start()

    pl.semaphore_wait(barrier, 26 + jnp.where(at_edge, 16, 0))

    @pl.when(at_edge)
    def _():
        @pl.loop(0, 16)
        def _(i):
            device = (((i // 2) % 4) * 4 + (1 - zh) * 2 + i % 2, x * 4 + served + i // 8)
            remote(ids_hbm, ids.at[h], ids_s.at[8 + i], ids_r.at[h], device).start()

        for i in range(2):
            device = (y * 4 + (1 - zh) * 2 + c, x * 4 + served + i)
            remote(offs_hbm, offs.at[zh], offs_s.at[i], offs_r.at[0], device).start()

    @pl.loop(1, 8)
    def _(i):
        remote(ids_hbm, ids.at[h], ids_s.at[i], ids_r.at[h], same_z(i)).start()

    for copy in local[2:6]:
        copy.wait()
    for d in (1, 3, 2):
        remote(
            wself.at[place], wself.at[place], wself_s.at[d], wself_r.at[place], y_peer(d)
        ).start()
    remote(wself.at[place], wself.at[place], wself_s.at[0], wself_r.at[place], sibling).start()

    local[6].wait()
    local[7].wait()
    ktab[...] = dot(tab[...], wk[...]).astype(BF16)
    local[8].wait()
    vtab[...] = dot(tab[...], wv[...]).astype(BF16)
    local[9].wait()
    qtab[...] = dot(tab[...], wq[...]).astype(BF16)

    local[0].wait()
    local[1].wait()

    @pl.loop(1, 8)
    def _(i):
        other = (place + i) % 8
        b = (other // 2) * 4 + zh * 2 + other % 2
        arrived(ids.at[b], ids_r.at[b])

    vocab_iota = lax.broadcasted_iota(jnp.int32, (256, 128), 0)
    row_iota = lax.broadcasted_iota(jnp.int32, (128, 128), 0)

    def earlier(half, seen):
        def add(i, seen):
            b = (i // 2) * 4 + half * 2 + i % 2
            return sum(
                (jnp.where(vocab_iota == ids[b, r : r + 1, :], 1.0, 0.0) for r in range(4)), seen
            )

        return lax.fori_loop(0, y * 2, add, seen)

    def token_hot(b):
        return jnp.concatenate(
            [jnp.where(vocab_iota == ids[b, r : r + 1, :], 1.0, 0.0).astype(BF16) for r in range(4)],
            axis=1,
        )

    def masks(b, offsets):
        blocks = []
        for r in range(4):
            places = row_iota + (b * TOKENS + r * 128)
            blocks.append(
                jnp.concatenate(
                    [
                        jnp.where(places <= offsets, 1.0, 0.0).astype(BF16),
                        jnp.where(places == offsets, 1.0, 0.0).astype(BF16),
                    ],
                    axis=1,
                )
            )
        return jnp.concatenate(blocks, axis=0)

    seen = earlier(zh, jnp.zeros((256, 128), F32))
    near_hots = [token_hot(y * 4 + zh * 2 + q) for q in range(2)]

    @pl.loop(0, 8)
    def _(i):
        b = (i // 2) * 4 + (1 - zh) * 2 + i % 2
        arrived(ids.at[b], ids_r.at[b])

    arrived(offs.at[1 - zh], offs_r.at[0])

    cross_output_weights(0)

    offsets = jnp.concatenate([offs[0], offs[1]], axis=1)
    counted = jnp.zeros((256, 256), F32)
    for q in range(2):
        counted += dot(near_hots[q], masks(y * 4 + zh * 2 + q, offsets))
        b = y * 4 + (1 - zh) * 2 + q
        counted += dot(token_hot(b), masks(b, offsets))
    seen = earlier(1 - zh, seen)

    counts = (counted[:, :128] + jnp.sum(seen, axis=1, keepdims=True)).T
    hot = counted[:, 128:].T.astype(BF16)
    lat_hot[...] = hot
    latent_queries = dot(hot, qtab[...]).astype(BF16)
    present = counts > 0.0
    heads = []
    for hd in range(2):
        cols = slice(hd * HEAD_DIM, (hd + 1) * HEAD_DIM)
        scores = dot_nt(latent_queries[:, cols], ktab[:, cols]) * SCALE
        scores = jnp.where(present, scores, -1e30)
        top = jnp.max(scores, axis=1, keepdims=True)
        weights = jnp.where(present, jnp.exp(scores - top), 0.0) * counts
        total = jnp.sum(weights, axis=1, keepdims=True)
        heads.append(dot(weights.astype(BF16), vtab[:, cols]) / total)
    ctx[...] = jnp.concatenate(heads, axis=1).astype(BF16)

    for copy in local[11:]:
        copy.wait()
    turn = 3 - 2 * (zl % 2)
    z_order = [(zl + e) % 4 for e in (2, turn, 4 - turn, 0)]
    for other in z_order:
        for e in (1, 0):
            b = ((x + e) % 2) * 4 + other
            part = dot(ctx[...], wo[b]).astype(BF16)
            send1[b] = part[:ROWS]
            send1[8 + b] = part[ROWS:]
            for d in (1, 3) if e else (2, 0):
                t = ((x + d) % 4) * 4 + other

                def send(t=t):
                    remote(send1.at[t], recv1.at[m], rs1_s.at[t], rs1_r.at[m], peer(t)).start()

                if d or other is not z_order[3]:
                    send()
    recv1[m] = send1[m]

    own_block = ((m % 8) // 2) * 4 + zh * 2 + m % 2
    total = dot(
        lat_hot[pl.ds(pl.multiple_of((m // 8) * ROWS, ROWS), ROWS)],
        tab[:, pl.ds(pl.multiple_of(own_block * WIDE, WIDE), WIDE)],
    )

    sums = jnp.zeros((ROWS, WIDE), F32)
    for other in reversed(z_order):
        for d in (0, 1, 3, 2):
            s = ((x + d) % 4) * 4 + other
            if d or other is not z_order[3]:
                arrived(recv1.at[s], rs1_r.at[s])
            sums += recv1[s].astype(F32)
    mid[m] = (total + sums).astype(BF16)

    order = (zl + 1 - 2 * (zl % 2), jnp.where(zl < 2, 2, 1), jnp.where(zl < 2, 3, 0))
    remote(mid.at[m], mid.at[m], ag_s.at[1], ag_r.at[m], (h, x * 4 + order[0])).start()
    for d in (1, 3, 2):
        remote(
            mid.at[m], mid.at[m], ag_s.at[4 + d], ag_r.at[m], (h, ((x + d) % 4) * 4 + zl)
        ).start()
    for e in (1, 2):
        remote(mid.at[m], mid.at[m], ag_s.at[1 + e], ag_r.at[m], (h, x * 4 + order[e])).start()

    for d in (1, 3, 2):
        remote(wso.at[h], wso.at[h], wso_s.at[2 + d], wso_r.at[h], y_peer(d)).start()
    spread_far(0)

    for e, other in enumerate(order):
        t = x * 4 + other
        arrived(mid.at[t], ag_r.at[t])
        for d in (1, 3, 2):
            remote(
                mid.at[t], mid.at[t], ag_s.at[8 + e * 4 + d], ag_r.at[t], (h, ((x + d) % 4) * 4 + zl)
            ).start()

    cross_output_weights(1)

    for d in (1, 3, 2):
        slot = ((y + d) % 4) * 2 + c
        arrived(wself.at[slot], wself_r.at[slot])
        remote(
            wself.at[slot], wself.at[slot], wself_s.at[4 + d], wself_r.at[slot], sibling
        ).start()

    local[10].wait()
    gain_rows[...] = gains[...].astype(F32)

    for d in range(4):
        slot = d * 2 + 1 - c
        arrived(wself.at[slot], wself_r.at[slot])

    squares = jnp.zeros((128, 128), F32)
    key_part = jnp.zeros((128, WIDE), F32)
    for other in (zl, *order):
        for e in range(2):
            b = e * 4 + other
            for r in range(2):

                @pl.when(x != e + 2 * r)
                def _(t=r * 8 + b):
                    arrived(mid.at[t], ag_r.at[t])

            rows = jnp.concatenate([mid[b], mid[8 + b]], axis=0).astype(F32)
            squares += rows[:, :128] * rows[:, :128] + rows[:, 128:] * rows[:, 128:]
            first = ((b // 2) * 4 + zh * 2 + b % 2) * 2
            gain = [gain_rows[pl.ds(first + i, 1), :] for i in range(2)]
            scaled = (rows * jnp.concatenate(gain, axis=1)).astype(BF16)
            left[b] = scaled
            key_part += dot(scaled, wself[b, 0])

    def keep(j, part):
        zsend[j, 0] = part[:ROWS].astype(BF16)
        zsend[j, 1] = part[ROWS:].astype(BF16)
        return part

    def project(j):
        part = dot(left[0], wself[0, j])
        for b in range(1, 8):
            part += dot(left[b], wself[b, j])
        return keep(j, part)

    def push(j):
        for r in range(2):
            k = j * 2 + r
            remote(zsend.at[j, r], zrecv.at[j, r], zx_s.at[k], zx_r.at[k], partner).start()

    def pushed(j):
        for r in range(2):
            left_here(zsend.at[j, r], zx_s.at[j * 2 + r])

    parts = [keep(0, key_part)]
    push(0)
    square = jnp.broadcast_to(jnp.sum(squares, axis=1, keepdims=True), (128, 128)).T
    ss_send[...] = square[0:8]
    remote(ss_send, ss_recv, zx_s.at[6], zx_r.at[6], partner).start()
    parts.append(project(1))
    push(1)
    parts.append(project(2))

    own_bit = (m // 2) % 2
    home = (m // 4) * 2 + m % 2

    @pl.when(own_bit == zh)
    def _():
        away = (1 - zh) * 8 + home
        remote(mid.at[away], resid, res_s.at[0], res_r.at[0], partner).start()
        resid[...] = mid[zh * 8 + home]

    spread_far(1)

    arrived(ss_recv, zx_r.at[6])
    square = ss_send[0:1] + ss_recv[0:1]
    norm = lax.rsqrt(square * (1.0 / 4096.0) + 1e-05)
    norm = jnp.broadcast_to(norm, (128, 128)).T
    norm = jnp.concatenate([norm, norm], axis=1)

    for d in (1, 3, 2):
        slot = ((y + d) % 4) * 4 + zh * 2 + c
        arrived(wso.at[slot], wso_r.at[slot])
    for d in range(4):
        slot = d * 4 + zh * 2 + c
        remote(wso.at[slot], wso.at[slot], wso_s.at[16 + d], wso_r.at[slot], sibling).start()

    def kv_block(j, slot, r):
        return kv.at[j, pl.ds(pl.multiple_of(slot * 128 + r * ROWS, ROWS), ROWS), :]

    def whole(j, r):
        arrived(zrecv.at[j, r], zx_r.at[j * 2 + r])
        rows = slice(r * ROWS, (r + 1) * ROWS)
        return ((parts[j][rows] + zrecv[j, r].astype(F32)) * norm[rows]).astype(BF16)

    for j in range(2):
        for r in range(2):
            block = kv_block(j, place, r)
            block[...] = whole(j, r)
            k = (j * 2 + r) * 8
            for d in (1, 3, 2):
                remote(block, block, kv_s.at[k + d], kv_r.at[k + place], y_peer(d)).start()
            remote(block, block, kv_s.at[k], kv_r.at[k + place], sibling).start()
        if j == 0:
            push(2)

    def pass_block(j, r):
        k = (j * 2 + r) * 8
        for d in (1, 3, 2):
            slot = ((y + d) % 4) * 2 + c
            block = kv_block(j, slot, r)
            arrived(block, kv_r.at[k + slot])
            remote(block, block, kv_s.at[k + 4 + d], kv_r.at[k + slot], sibling).start()

    def wait_block(j, r):
        for d in range(4):
            slot = d * 2 + 1 - c
            arrived(kv_block(j, slot, r), kv_r.at[(j * 2 + r) * 8 + slot])

    pass_block(0, 0)
    pass_block(0, 1)
    queries[0:ROWS] = whole(2, 0)
    queries[ROWS:] = whole(2, 1)

    for d in (1, 3, 2):
        slot = ((y + d) % 4) * 4 + (1 - zh) * 2 + c
        for k in range(2):
            arrived(half_slot(slot, k), wso_r.at[16 + slot * 2 + k])
    for d in range(4):
        slot = d * 4 + (1 - zh) * 2 + c
        remote(wso.at[slot], wso.at[slot], wso_s.at[20 + d], wso_r.at[slot], sibling).start()

    wait_block(0, 0)
    wait_block(0, 1)

    key_lane = lax.broadcasted_iota(jnp.int32, (128, 1024), 1)
    key_in = key_lane % 128
    key_place = (
        (key_lane // 256) * 256 + ((key_lane // 128) % 2) * 64 + (key_in // 64) * 128 + key_in % 64
    )
    query_row = lax.broadcasted_iota(jnp.int32, (128, 1024), 0)
    query_place = y * 256 + c * 64 + (query_row // 64) * 128 + query_row % 64
    allowed = key_place <= query_place
    spread, totals = [], []
    for hd in range(2):
        cols = slice(hd * HEAD_DIM, (hd + 1) * HEAD_DIM)
        scores = dot_nt(queries[:, cols], kv[0, :, cols]) * SCALE
        scores = jnp.where(allowed, scores, -1e30)
        top = jnp.max(scores, axis=1, keepdims=True)
        weights = jnp.where(allowed, jnp.exp(scores - top), 0.0)
        totals.append(jnp.sum(weights, axis=1, keepdims=True))
        spread.append(weights.astype(BF16))

    pass_block(1, 0)
    pass_block(1, 1)

    wait_block(1, 0)
    wait_block(1, 1)

    heads = []
    for hd in range(2):
        cols = slice(hd * HEAD_DIM, (hd + 1) * HEAD_DIM)
        heads.append(dot(spread[hd], kv[1, :, cols]) / totals[hd])
    ctx[...] = jnp.concatenate(heads, axis=1).astype(BF16)

    for d in range(4):
        for half in range(2):
            slot = d * 4 + half * 2 + 1 - c
            arrived(wso.at[slot], wso_r.at[slot])

    def self_part(t):
        rows = pl.ds(pl.multiple_of(half_of(t % 4) * ROWS, ROWS), ROWS)
        return dot(ctx[rows, :], wso[t]).astype(BF16)

    for other in z_order:
        for d in (2, 1, 3, 0):
            t = ((x + d) % 4) * 4 + other
            if d or other is not z_order[3]:
                send2[t] = self_part(t)
                remote(send2.at[t], recv2.at[m], rs2_s.at[t], rs2_r.at[m], peer(t)).start()
    recv2[m] = self_part(m)

    @pl.when(own_bit != zh)
    def _():
        arrived(resid, res_r.at[0])

    sums = resid[...].astype(F32)
    for other in reversed(z_order):
        for d in (0, 1, 3, 2):
            s = ((x + d) % 4) * 4 + other
            if d or other is not z_order[3]:
                arrived(recv2.at[s], rs2_r.at[s])
            sums += recv2[s].astype(F32)
    out_ref[...] = sums.astype(BF16)

    @pl.loop(1, 16)
    def _(i):
        s = (m + i) % 16
        left_here(send1.at[s], rs1_s.at[s])
        left_here(send2.at[s], rs2_s.at[s])

    @pl.when(at_edge)
    def _():
        @pl.loop(0, 16)
        def _(i):
            left_here(ids.at[h], ids_s.at[8 + i])

        for i in range(2):
            left_here(offs.at[0], offs_s.at[i])

    @pl.loop(1, 8)
    def _(i):
        left_here(ids.at[h], ids_s.at[i])

    @pl.loop(0, 8)
    def _(i):
        @pl.when(i != 4)
        def _():
            left_here(wself.at[0], wself_s.at[i])
            for k in range(4):
                left_here(kv_block(0, 0, 0), kv_s.at[k * 8 + i])

    for i in (0, 1, 7, 8, 9, 11, 12, 13):
        left_here(half_slot(0, 0), wso_s.at[i])
    for i in (3, 4, 5, 16, 17, 18, 19, 20, 21, 22, 23):
        left_here(wso.at[0], wso_s.at[i])

    for i in (1, 2, 3, 5, 6, 7, 9, 10, 11, 13, 14, 15, 17, 18, 19):
        left_here(mid.at[0], ag_s.at[i])
    pushed(0)
    pushed(1)
    pushed(2)
    left_here(ss_send, zx_s.at[6])

    @pl.when(own_bit == zh)
    def _():
        left_here(resid, res_s.at[0])


def per_device(
    history_ids, latent_offsets, byte_table, w_query, w_key, w_value, w_out, norm_gain,
    w_self_query, w_self_key, w_self_value, w_self_out,
):
    vmem = pl.BlockSpec(memory_space=pltpu.VMEM)
    hbm = pl.BlockSpec(memory_space=pl.ANY)
    dma = pltpu.SemaphoreType.DMA
    scratch = [
        pltpu.VMEM((16, 4, 128), jnp.int32),
        pltpu.VMEM((2, 1, 64), jnp.int32),
        pltpu.VMEM((32, 128), BF16),
        pltpu.VMEM((32, 128), F32),
        pltpu.VMEM((256, 4096), BF16),
        pltpu.VMEM((4096, 256), BF16),
        pltpu.VMEM((4096, 256), BF16),
        pltpu.VMEM((4096, 256), BF16),
        pltpu.VMEM((8, 256, 256), BF16),
        pltpu.VMEM((8, 3, 256, 256), BF16),
        pltpu.VMEM((16, 256, 256), BF16),
        pltpu.VMEM((256, 256), BF16),
        pltpu.VMEM((256, 256), BF16),
        pltpu.VMEM((256, 256), BF16),
        pltpu.VMEM((128, 256), BF16),
        pltpu.VMEM((16, ROWS, WIDE), BF16),
        pltpu.VMEM((16, ROWS, WIDE), BF16),
        pltpu.VMEM((16, ROWS, WIDE), BF16),
        pltpu.VMEM((8, 128, WIDE), BF16),
        pltpu.VMEM((3, 2, ROWS, WIDE), BF16),
        pltpu.VMEM((3, 2, ROWS, WIDE), BF16),
        pltpu.VMEM((8, 128), F32),
        pltpu.VMEM((8, 128), F32),
        pltpu.VMEM((2, 1024, WIDE), BF16),
        pltpu.VMEM((128, WIDE), BF16),
        pltpu.VMEM((128, WIDE), BF16),
        pltpu.VMEM((16, ROWS, WIDE), BF16),
        pltpu.VMEM((16, ROWS, WIDE), BF16),
        pltpu.VMEM((ROWS, WIDE), BF16),
    ] + [dma((n,)) for n in (
        19, 24, 16, 8, 8, 24, 48, 16, 16, 20, 16, 7, 7, 32, 32, 16, 16, 1, 1, 2, 1
    )]
    return pl.pallas_call(
        kernel,
        out_shape=jax.ShapeDtypeStruct((ROWS, WIDE), BF16),
        in_specs=[hbm] * 12,
        out_specs=vmem,
        scratch_shapes=scratch,
        compiler_params=pltpu.CompilerParams(
            collective_id=0, has_side_effects=True, vmem_limit_bytes=56 * 1024 * 1024
        ),
        cost_estimate=pl.CostEstimate(
            flops=5_000_000_000, bytes_accessed=12_000_000, transcendentals=400_000
        ),
    )(
        history_ids.reshape(4, 128), latent_offsets.reshape(1, 64), norm_gain.reshape(32, 128),
        byte_table, w_query, w_key, w_value, w_out,
        w_self_query, w_self_key, w_self_value, w_self_out,
    )


def solution(mesh):
    return jax.shard_map(
        per_device,
        mesh=mesh,
        in_specs=(
            P("hist"),
            P("hist"),
            P(),
            P(None, "mp"),
            P(None, "mp"),
            P(None, "mp"),
            P("mp", None),
            P(),
            P("hist", "mp"),
            P("hist", "mp"),
            P("hist", "mp"),
            P("mp", "hist"),
        ),
        out_specs=P("hist", "mp"),
        check_vma=False,
    )
```
